512 devices in a mesh: seq: 64 (over z, x), head: 8 (over y, core).
Axes of the slice: x: 4, y: 4, z: 16, core: 2. Of those that a mesh axis runs over, the one named last changes fastest.
Arguments:
- queries: bfloat16 [32768, 2048], P(('seq', 'head')), may hold values from -6 to 6
- keys: bfloat16 [32768, 2048], P(('seq', 'head')), may hold values from -6 to 6
- values: bfloat16 [32768, 4096], P(('seq', 'head')), may hold values from -6 to 6
- in_gate: float32 [8, 32768], P('head', 'seq'), may hold values from -8 to 130
- forget_gate: float32 [8, 32768], P('head', 'seq'), may hold values from -0.1 to 14
- out_gate: bfloat16 [32768, 4096], P(('seq', 'head')), may hold values from -6 to 6
Outputs:
- layer_output: bfloat16 [32768, 4096], P(('seq', 'head'))
The draws below stay inside these ranges and needn't reach their ends.
All inputs are finite; a program needn't handle non-finite values.
Results may differ from the reference program's by a relative error of at most 0.0065.
Values may be sent and summed in bfloat16 or wider, within the bound.
A program may use at most 128 MiB of HBM per device.

```python
import math
import jax
import jax.numpy as jnp
from jax import lax

LSTM_HEAD_COUNT = 8
DK = 256
DV = 512
BLOCK = 512
TOKENS = 32768
N_SEQ = 64


def draw_in_gate(key, part):
    key = jax.random.fold_in(key, 11)
    base_key = jax.random.fold_in(key, 0)
    base = jax.random.normal(base_key, (LSTM_HEAD_COUNT, TOKENS), jnp.float32) * 2.0
    return jnp.clip(base, -7.0, 7.0)


def draw_forget_gate(key, part):
    key = jax.random.fold_in(key, 23)
    permutation_key, token_random_key, block_random_key, location_key, spike_random_key = jax.random.split(key, 5)
    order = jax.random.permutation(permutation_key, LSTM_HEAD_COUNT)
    slow_count = LSTM_HEAD_COUNT // 2
    slow = order < slow_count
    slow_rate = 0.25 * math.log(10.0) / TOKENS
    fast_rate = 1.0 / 40.0
    head_rate = jnp.where(slow, slow_rate, fast_rate)
    token_factor = jnp.exp(jax.random.uniform(token_random_key, (LSTM_HEAD_COUNT, TOKENS), jnp.float32, -0.7, 0.7))
    block_factor = jnp.exp(jax.random.uniform(block_random_key, (LSTM_HEAD_COUNT, TOKENS // BLOCK, 1), jnp.float32, -0.7, 0.7))
    block_factor = jnp.broadcast_to(block_factor, (LSTM_HEAD_COUNT, TOKENS // BLOCK, BLOCK)).reshape(LSTM_HEAD_COUNT, TOKENS)
    event_probability = head_rate[:, None] * token_factor * block_factor
    spots = jax.random.randint(location_key, (LSTM_HEAD_COUNT, 3), 0, TOKENS)
    spike_event = jax.random.uniform(spike_random_key, (LSTM_HEAD_COUNT, 3), jnp.float32, 0.22, 0.69)
    places = jnp.arange(TOKENS)
    spike_flags = places[None, None, :] == spots[:, :, None]
    spike_probability = jnp.max(jnp.where(spike_flags, spike_event[:, :, None], 0.0), axis=1)
    event_probability = jnp.maximum(event_probability, spike_probability)
    return -jnp.log(jnp.expm1(event_probability))


def shard_levels(stream_key, extent, cuts, low, high):
    loudness, own = 1.0, jax.random.fold_in(stream_key, 6)
    for position, parts in cuts:
        draws = jnp.exp(jax.random.uniform(jax.random.fold_in(own, position), (parts,), jnp.float32, low / len(cuts), high / len(cuts)))
        loudness = loudness * jnp.repeat(draws, extent[position] // parts).reshape([-1 if axis == position else 1 for axis in range(len(extent))])
    return loudness


def centred(own_key, dims, deviation, limit, shards=(), held_as=jnp.bfloat16):
    drawn = jax.random.normal(own_key, dims, jnp.float32) * deviation
    if len(shards) > 0:
        drawn = shard_levels(own_key, dims, shards, -0.22, 0.18) * drawn
    return jnp.clip(drawn, min=-limit, max=limit).astype(held_as)


def setup_inputs(seed: int = 0) -> dict:
    splits = jax.random.split(jax.random.key(seed), 7)
    return {
        "queries": centred(splits[0], (TOKENS, LSTM_HEAD_COUNT * DK), 1.0, 6.0, ((0, 512),)),
        "keys": centred(splits[1], (TOKENS, LSTM_HEAD_COUNT * DK), 1.0, 6.0, ((0, 512),)),
        "values": centred(splits[2], (TOKENS, LSTM_HEAD_COUNT * DV), 1.0, 6.0, ((0, 512),)),
        "in_gate": draw_in_gate(jax.random.fold_in(splits[6], 71), 0),
        "forget_gate": draw_forget_gate(jax.random.fold_in(splits[6], 71), 0),
        "out_gate": centred(splits[5], (TOKENS, LSTM_HEAD_COUNT * DV), 1.5, 6.0, ((0, 512),)),
    }


def block_pass(carried, inputs):
    memory, normal, peak = carried
    query_blk, key_blk, value_blk, keep_blk, gate_blk = inputs
    scale = DK ** -0.5
    within = jnp.cumsum(keep_blk)
    decay_total = within[-1]
    since_end = decay_total - within + gate_blk
    peak_own = jnp.max(since_end)
    weight = jnp.exp(since_end - peak_own)
    key_wide = key_blk.astype(jnp.float32)
    weighted_keys = (weight[:, None] * key_wide).astype(jnp.bfloat16)
    memory_own = jnp.dot(weighted_keys.T, value_blk, preferred_element_type=jnp.float32)
    normal_own = jnp.sum(weight[:, None] * key_wide, axis=0)
    entry_log = within + peak
    local_log = within[:, None] - within[None, :] + gate_blk[None, :]
    positions = jnp.arange(BLOCK)
    causal = positions[None, :] <= positions[:, None]
    local_log = jnp.where(causal, local_log, -jnp.inf)
    peak_row = jnp.maximum(entry_log, jnp.max(local_log, axis=1))
    scores = jnp.dot(query_blk, key_blk.T, preferred_element_type=jnp.float32) * scale
    mixing = jnp.exp(local_log - peak_row[:, None]) * scores
    query_expanded = query_blk.astype(jnp.float32) * scale
    entry_scale = jnp.exp(entry_log - peak_row)
    numerator = jnp.dot(mixing.astype(jnp.bfloat16), value_blk, preferred_element_type=jnp.float32)
    numerator = numerator + entry_scale[:, None] * jnp.dot(query_expanded, memory, precision=lax.Precision.HIGHEST)
    denominator = jnp.sum(mixing, axis=1) + entry_scale * jnp.dot(query_expanded, normal, precision=lax.Precision.HIGHEST)
    hidden = (numerator / jnp.maximum(jnp.abs(denominator), 1.0)[:, None]).astype(jnp.bfloat16)
    peak_next = jnp.maximum(decay_total + peak, peak_own)
    scale_old = jnp.exp(decay_total + peak - peak_next)
    scale_new = jnp.exp(peak_own - peak_next)
    memory_next = scale_old * memory + scale_new * memory_own
    normal_next = scale_old * normal + scale_new * normal_own
    return (memory_next, normal_next, peak_next), hidden


def head_pass(inputs):
    start = (jnp.zeros((DK, DV), jnp.float32), jnp.zeros((DK,), jnp.float32), jnp.full((), -1.0e30, jnp.float32))
    final_state, hidden = lax.scan(block_pass, start, inputs)
    return hidden


def reference(queries, keys, values, in_gate, forget_gate, out_gate):
    query_heads = queries.reshape(N_SEQ, BLOCK, LSTM_HEAD_COUNT, DK).transpose(2, 0, 1, 3)
    key_heads = keys.reshape(N_SEQ, BLOCK, LSTM_HEAD_COUNT, DK).transpose(2, 0, 1, 3)
    value_heads = values.reshape(N_SEQ, BLOCK, LSTM_HEAD_COUNT, DV).transpose(2, 0, 1, 3)
    log_keep = jax.nn.log_sigmoid(forget_gate).reshape(LSTM_HEAD_COUNT, N_SEQ, BLOCK)
    gate_heads = in_gate.reshape(LSTM_HEAD_COUNT, N_SEQ, BLOCK)
    hidden = lax.map(head_pass, (query_heads, key_heads, value_heads, log_keep, gate_heads))
    hidden = hidden.transpose(1, 2, 0, 3).reshape(TOKENS, LSTM_HEAD_COUNT * DV)
    gated = jax.nn.sigmoid(out_gate.astype(jnp.float32)) * hidden.astype(jnp.float32)
    return gated.astype(jnp.bfloat16)
```

```python
import functools

import jax
import jax.numpy as jnp
from jax import lax
from jax.experimental import pallas as pl
from jax.experimental.pallas import tpu as pltpu
from jax.sharding import PartitionSpec as P

MESH = pl.DeviceIdType.MESH
NEG_FILL = -1e30
MEMBERS = 16
CHUNKS = 2
TILE = 128


def kernel(
    sizes,
    q_ref,
    k_ref,
    v_ref,
    ig_ref,
    fg_ref,
    ret_ref,
    qbuf,
    kbuf,
    vbuf,
    wkt,
    within_col,
    weight_col,
    local_max,
    scores,
    mixing,
    entry_rate,
    local_out,
    hdr,
    hdr_all,
    hdr_total,
    hdr_total_all,
    coef_local,
    coef_full,
    entry,
    coef_total,
    mown,
    mrecv,
    usend,
    urecv,
    isend,
    irecv,
    hid,
    send_sem,
    recv_sem,
    relay_sem,
):
    n_seq, n_head = sizes
    n_group = n_seq // MEMBERS
    tok = q_ref.shape[0]
    rows, key_dim = kbuf.shape
    width = vbuf.shape[2]
    value_dim = width * CHUNKS
    part = key_dim // MEMBERS
    seq = lax.axis_index("seq")
    head = lax.axis_index("head")
    me = lax.rem(seq, MEMBERS)
    group = seq // MEMBERS
    base = group * MEMBERS
    head_row = pl.multiple_of(head * tok, tok)

    K, Q, HDR, HDRT = 0, 1, 2, 3
    V, A, B, C, R = (4 + CHUNKS * i for i in range(5))

    def member(j):
        return base + lax.rem(me + j, MEMBERS)

    def stride(j):
        return lax.rem(seq + MEMBERS * j, n_seq)

    def peer(j):
        return lax.rem(head + j, n_head)

    def put(src, dst, which, device):
        pltpu.make_async_remote_copy(
            src_ref=src,
            dst_ref=dst,
            send_sem=send_sem.at[which],
            recv_sem=recv_sem.at[which],
            device_id=device,
            device_id_type=MESH,
        ).start()

    def arrived(ref, which):
        pltpu.make_async_copy(ref, ref, recv_sem.at[which]).wait()

    def sent(ref, which):
        pltpu.make_async_copy(ref, ref, send_sem.at[which]).wait()

    barrier = pltpu.get_barrier_semaphore()
    for j in range(1, n_head):
        pl.semaphore_signal(barrier, inc=1, device_id=(seq, peer(j)), device_id_type=MESH)
    for j in range(1, MEMBERS):
        pl.semaphore_signal(barrier, inc=1, device_id=(member(j), head), device_id_type=MESH)
    for j in (1, n_group - 1):
        pl.semaphore_signal(barrier, inc=1, device_id=(stride(j), head), device_id_type=MESH)

    def local(src, dst, which):
        pltpu.make_async_copy(src, dst, recv_sem.at[which]).start()

    def key_cols(h):
        return pl.ds(pl.multiple_of(h * key_dim, key_dim), key_dim)

    def value_cols(h, c):
        return pl.ds(pl.multiple_of(h * value_dim + c * width, width), width)

    my_rows = pl.ds(head_row, tok)
    local(k_ref.at[:, key_cols(head)], kbuf.at[my_rows], K)
    for c in range(CHUNKS):
        local(v_ref.at[:, value_cols(head, c)], vbuf.at[c, my_rows], V + c)
    local(q_ref.at[:, key_cols(head)], qbuf.at[my_rows], Q)

    gate = ig_ref[...]
    forget = fg_ref[...]
    log_keep = jnp.minimum(forget, 0.0) - jnp.log1p(jnp.exp(-jnp.abs(forget)))
    lane = lax.broadcasted_iota(jnp.int32, (8, rows), 1)
    within_row = jnp.broadcast_to(log_keep, (8, rows))
    step = 1
    while step < rows:
        within_row = within_row + jnp.where(lane >= step, pltpu.roll(within_row, step, 1), 0.0)
        step *= 2
    within_row = within_row[0:1, :]
    decay = within_row[:, rows - 1 : rows]
    gate_less = gate - within_row

    def gate_tile(i, peak):
        at = pl.ds(pl.multiple_of(i * TILE, TILE), TILE)
        t = lax.broadcasted_iota(jnp.int32, (TILE, rows), 0) + i * TILE
        s = lax.broadcasted_iota(jnp.int32, (TILE, rows), 1)
        col = jnp.sum(jnp.where(s <= t, log_keep, 0.0), axis=1, keepdims=True)
        own_gate = jnp.sum(jnp.where(s == t, gate, 0.0), axis=1, keepdims=True)
        since = decay - col + own_gate
        within_col[at, :] = col
        weight_col[at, :] = since
        local_max[at, :] = col + jnp.max(
            jnp.where(s <= t, gate_less, NEG_FILL), axis=1, keepdims=True
        )
        return jnp.maximum(peak, jnp.max(since, axis=0, keepdims=True))

    peak_own = lax.fori_loop(
        0, rows // TILE, gate_tile, jnp.full((1, 1), -jnp.inf, jnp.float32)
    )
    hdr[...] = jnp.zeros_like(hdr)
    hdr[0:1, :] = jnp.broadcast_to(decay, (1, 128))
    hdr[1:2, :] = jnp.broadcast_to(peak_own, (1, 128))
    hdr_total[...] = jnp.zeros_like(hdr_total)
    hdr_total_all[group] = jnp.zeros(hdr_total.shape, jnp.float32)
    for c in range(CHUNKS):
        urecv[c, group] = jnp.zeros(urecv.shape[2:], urecv.dtype)

    pl.semaphore_wait(barrier, n_head - 1 + MEMBERS - 1 + 2)
    pl.semaphore_signal(relay_sem, inc=1, device_id=(stride(1), head), device_id_type=MESH)

    for j in range(1, n_head):
        h = peer(j)
        put(k_ref.at[:, key_cols(h)], kbuf.at[my_rows], K, (seq, h))
    for c in range(CHUNKS):
        for j in range(1, n_head):
            h = peer(j)
            put(v_ref.at[:, value_cols(h, c)], vbuf.at[c, my_rows], V + c, (seq, h))
    for j in range(1, n_head):
        h = peer(j)
        put(q_ref.at[:, key_cols(h)], qbuf.at[my_rows], Q, (seq, h))

    arrived(kbuf, K)

    def key_tile(i, normal):
        at = pl.ds(pl.multiple_of(i * TILE, TILE), TILE)
        weight = jnp.exp(weight_col[at, :] - peak_own)
        weighted = weight * kbuf[at, :].astype(jnp.float32)
        wkt[:, at] = weighted.T.astype(jnp.bfloat16)
        return normal + jnp.sum(weighted, axis=0, keepdims=True)

    normal_own = lax.fori_loop(
        0, rows // TILE, key_tile, jnp.zeros((1, key_dim), jnp.float32)
    )
    for i in range(key_dim // 128):
        hdr[2 + i : 3 + i, :] = normal_own[:, i * 128 : (i + 1) * 128]
    hdr_all[me] = hdr[...]
    for j in range(1, MEMBERS):
        put(hdr, hdr_all.at[me], HDR, (member(j), head))

    for c in range(CHUNKS):
        arrived(vbuf.at[c], V + c)
        own = jnp.dot(wkt[...], vbuf[c], preferred_element_type=jnp.float32)
        mown[c] = own.astype(jnp.bfloat16).reshape(MEMBERS, part, width)
        for j in range(1, MEMBERS):
            g = lax.rem(me + j, MEMBERS)
            put(mown.at[c, g], mrecv.at[c, me], A + c, (base + g, head))
        mrecv[c, me] = mown[c, me]

    norm_rows = slice(2, 2 + key_dim // 128)
    no_peak = jnp.full((1, 128), NEG_FILL, jnp.float32)
    no_norm = jnp.zeros((key_dim // 128, 128), jnp.float32)

    arrived(hdr_all.at[pl.ds(0, MEMBERS - 1)], HDR)
    peak, norm, total = no_peak, no_norm, jnp.zeros((1, 128), jnp.float32)
    for g in range(MEMBERS):
        d, p = hdr_all[g, 0:1, :], hdr_all[g, 1:2, :]
        new = jnp.maximum(d + peak, p)
        older, newer = jnp.exp(d + peak - new), jnp.exp(p - new)
        coef_local[g, 0:1, :] = older
        coef_local[g, 1:2, :] = newer
        norm = older * norm + newer * hdr_all[g, norm_rows, :]
        peak, total = new, total + d
    hdr_total[0:1, :] = total
    hdr_total[1:2, :] = peak
    hdr_total[norm_rows, :] = norm
    pl.semaphore_wait(relay_sem, 1)
    for j in range(1, n_group):
        put(hdr_total, hdr_total_all.at[group], HDRT, (stride(j), head))

    arrived(qbuf, Q)
    scale = key_dim ** (-0.5)

    def score_tile(i, carry):
        at = pl.ds(pl.multiple_of(i * TILE, TILE), TILE)
        scores[at, :] = lax.dot_general(
            qbuf[at, :], kbuf[...], (((1,), (1,)), ((), ())), preferred_element_type=jnp.float32
        )
        return carry

    lax.fori_loop(0, rows // TILE, score_tile, 0)

    def wide(row):
        return jnp.concatenate([row] * (width // 128), axis=1)

    for c in range(CHUNKS):
        arrived(mrecv.at[c, pl.ds(0, MEMBERS - 1)], A + c)
        state = jnp.zeros((part, width), jnp.float32)
        for g in range(MEMBERS):
            state = (
                wide(coef_local[g, 0:1, :]) * state
                + wide(coef_local[g, 1:2, :]) * mrecv[c, g].astype(jnp.float32)
            )
        usend[c] = state.astype(jnp.bfloat16)
        for j in range(1, n_group):
            put(usend.at[c], urecv.at[c, group], B + c, (stride(j), head))

    arrived(hdr_total_all.at[pl.ds(0, n_group - 1)], HDRT)
    peak, norm = no_peak, no_norm
    for j in range(n_group - 1):
        d, p = hdr_total_all[j, 0:1, :], hdr_total_all[j, 1:2, :]
        new = jnp.maximum(d + peak, p)
        used = j < group
        older = jnp.where(used, jnp.exp(d + peak - new), 1.0)
        newer = jnp.where(used, jnp.exp(p - new), 0.0)
        coef_total[j, 0:1, :] = older
        coef_total[j, 1:2, :] = newer
        norm = jnp.where(used, older * norm + newer * hdr_total_all[j, norm_rows, :], norm)
        peak = jnp.where(used, new, peak)
    for g in range(MEMBERS):
        entry[g, 1:2, :] = peak
        entry[g, norm_rows, :] = norm
        d, p = hdr_all[g, 0:1, :], hdr_all[g, 1:2, :]
        new = jnp.maximum(d + peak, p)
        older, newer = jnp.exp(d + peak - new), jnp.exp(p - new)
        coef_full[g, 0:1, :] = older
        coef_full[g, 1:2, :] = newer
        norm = older * norm + newer * hdr_all[g, norm_rows, :]
        peak = new

    my_entry = entry[me]
    peak_in = my_entry[1:2, 0:1]
    normal_in = jnp.concatenate(
        [my_entry[2 + i : 3 + i, :] for i in range(key_dim // 128)], axis=1
    )

    def mixing_tile(i, carry):
        at = pl.ds(pl.multiple_of(i * TILE, TILE), TILE)
        t = lax.broadcasted_iota(jnp.int32, (TILE, rows), 0) + i * TILE
        s = lax.broadcasted_iota(jnp.int32, (TILE, rows), 1)
        col = within_col[at, :]
        entry_log = col + peak_in
        peak_row = jnp.maximum(entry_log, local_max[at, :])
        logs = jnp.where(s <= t, (col - peak_row) + gate_less, NEG_FILL)
        mix = jnp.exp(logs) * (scores[at, :] * scale)
        mixing[at, :] = mix.astype(jnp.bfloat16)
        rate = jnp.exp(entry_log - peak_row)
        from_normal = jnp.sum(
            qbuf[at, :].astype(jnp.float32) * normal_in, axis=1, keepdims=True
        )
        below = jnp.sum(mix, axis=1, keepdims=True) + rate * (from_normal * scale)
        inverse = 1.0 / jnp.maximum(jnp.abs(below), 1.0)
        entry_rate[at, 0:1] = rate * inverse * scale
        entry_rate[at, 1:2] = inverse
        return carry

    lax.fori_loop(0, rows // TILE, mixing_tile, 0)

    for c in range(CHUNKS):
        arrived(urecv.at[c, pl.ds(0, n_group - 1)], B + c)
        state = jnp.zeros((part, width), jnp.float32)
        for j in range(n_group - 1):
            state = jnp.where(
                j < group,
                wide(coef_total[j, 0:1, :]) * state
                + wide(coef_total[j, 1:2, :]) * urecv[c, j].astype(jnp.float32),
                state,
            )
        for g in range(MEMBERS):
            isend[c, g] = state.astype(jnp.bfloat16)
            state = (
                wide(coef_full[g, 0:1, :]) * state
                + wide(coef_full[g, 1:2, :]) * mrecv[c, g].astype(jnp.float32)
            )
        my_part = pl.ds(pl.multiple_of(me * part, part), part)
        for j in range(1, MEMBERS):
            g = lax.rem(me + j, MEMBERS)
            put(isend.at[c, g], irecv.at[c, my_part], C + c, (base + g, head))
        irecv[c, my_part] = isend[c, me]

    def local_tile(i, carry):
        at = pl.ds(pl.multiple_of(i * TILE, TILE), TILE)
        for c in range(CHUNKS):
            local_out[c, at, :] = entry_rate[at, 1:2] * jnp.dot(
                mixing[at, :], vbuf[c], preferred_element_type=jnp.float32
            )
        return carry

    lax.fori_loop(0, rows // TILE, local_tile, 0)

    for c in range(CHUNKS):
        arrived(irecv.at[c, pl.ds(0, key_dim - part)], C + c)

        def out_tile(i, carry):
            at = pl.ds(pl.multiple_of(i * TILE, TILE), TILE)
            from_memory = jnp.dot(
                qbuf[at, :], irecv[c], preferred_element_type=jnp.float32
            )
            hid[c, at, :] = (
                local_out[c, at, :] + entry_rate[at, 0:1] * from_memory
            ).astype(jnp.bfloat16)
            return carry

        lax.fori_loop(0, rows // TILE, out_tile, 0)
        for j in range(1, n_head):
            h = peer(j)
            put(
                hid.at[c, pl.ds(pl.multiple_of(h * tok, tok), tok)],
                ret_ref.at[:, value_cols(head, c)],
                R + c,
                (seq, h),
            )
        local(hid.at[c, my_rows], ret_ref.at[:, value_cols(head, c)], R + c)

    for c in range(CHUNKS):
        arrived(hid.at[c], R + c)

    peers_rows = pl.ds(0, rows - tok)
    sent(kbuf.at[peers_rows], K)
    sent(qbuf.at[peers_rows], Q)
    sent(hdr_all.at[pl.ds(0, MEMBERS - 1)], HDR)
    sent(hdr_total_all.at[pl.ds(0, n_group - 1)], HDRT)
    for c in range(CHUNKS):
        sent(vbuf.at[c, peers_rows], V + c)
        sent(mrecv.at[c, pl.ds(0, MEMBERS - 1)], A + c)
        sent(urecv.at[c, pl.ds(0, n_group - 1)], B + c)
        sent(irecv.at[c, pl.ds(0, key_dim - part)], C + c)
        sent(hid.at[c, peers_rows], R + c)


def per_device(n_seq, n_head, queries, keys, values, in_gate, forget_gate, out_gate):
    tok = queries.shape[0]
    rows = tok * n_head
    key_dim = queries.shape[1] // n_head
    value_dim = values.shape[1] // n_head
    width = value_dim // CHUNKS
    part = key_dim // MEMBERS
    n_group = n_seq // MEMBERS
    bf16, f32 = jnp.bfloat16, jnp.float32
    scratch = [
        pltpu.VMEM((rows, key_dim), bf16),
        pltpu.VMEM((rows, key_dim), bf16),
        pltpu.VMEM((CHUNKS, rows, width), bf16),
        pltpu.VMEM((key_dim, rows), bf16),
        pltpu.VMEM((rows, 1), f32),
        pltpu.VMEM((rows, 1), f32),
        pltpu.VMEM((rows, 1), f32),
        pltpu.VMEM((rows, rows), f32),
        pltpu.VMEM((rows, rows), bf16),
        pltpu.VMEM((rows, 2), f32),
        pltpu.VMEM((CHUNKS, rows, width), f32),
        pltpu.VMEM((8, 128), f32),
        pltpu.VMEM((MEMBERS, 8, 128), f32),
        pltpu.VMEM((8, 128), f32),
        pltpu.VMEM((n_group, 8, 128), f32),
        pltpu.VMEM((MEMBERS, 8, 128), f32),
        pltpu.VMEM((MEMBERS, 8, 128), f32),
        pltpu.VMEM((MEMBERS, 8, 128), f32),
        pltpu.VMEM((n_group, 8, 128), f32),
        pltpu.VMEM((CHUNKS, MEMBERS, part, width), bf16),
        pltpu.VMEM((CHUNKS, MEMBERS, part, width), bf16),
        pltpu.VMEM((CHUNKS, part, width), bf16),
        pltpu.VMEM((CHUNKS, n_group, part, width), bf16),
        pltpu.VMEM((CHUNKS, MEMBERS, part, width), bf16),
        pltpu.VMEM((CHUNKS, key_dim, width), bf16),
        pltpu.VMEM((CHUNKS, rows, width), bf16),
        pltpu.SemaphoreType.DMA((4 + 5 * CHUNKS,)),
        pltpu.SemaphoreType.DMA((4 + 5 * CHUNKS,)),
        pltpu.SemaphoreType.REGULAR,
    ]
    anywhere = pl.BlockSpec(memory_space=pl.ANY)
    vmem = pl.BlockSpec(memory_space=pltpu.VMEM)
    returned = pl.pallas_call(
        functools.partial(kernel, (n_seq, n_head)),
        out_shape=jax.ShapeDtypeStruct((tok, n_head * value_dim), bf16),
        in_specs=[anywhere, anywhere, anywhere, vmem, vmem],
        out_specs=anywhere,
        scratch_shapes=scratch,
        compiler_params=pltpu.CompilerParams(
            collective_id=0, has_side_effects=True, vmem_limit_bytes=40 * 2**20
        ),
    )(queries, keys, values, in_gate, forget_gate)
    gated = jax.nn.sigmoid(out_gate.astype(f32)) * returned.astype(f32)
    return gated.astype(bf16)


def solution(mesh):
    return jax.shard_map(
        functools.partial(per_device, mesh.shape["seq"], mesh.shape["head"]),
        mesh=mesh,
        in_specs=(
            P(("seq", "head"), None),
            P(("seq", "head"), None),
            P(("seq", "head"), None),
            P("head", "seq"),
            P("head", "seq"),
            P(("seq", "head"), None),
        ),
        out_specs=P(("seq", "head"), None),
        check_vma=False,
    )
```

```python
import functools

import jax
import jax.numpy as jnp
from jax import lax
from jax.experimental import pallas as pl
from jax.experimental.pallas import tpu as pltpu
from jax.sharding import PartitionSpec as P

MESH = pl.DeviceIdType.MESH
NEG_FILL = -1e30
MEMBERS = 16
CHUNKS = 2
TILE = 128


def kernel(
    sizes,
    q_ref,
    k_ref,
    v_ref,
    ig_ref,
    fg_ref,
    ret_ref,
    gates,
    qbuf,
    kbuf,
    vbuf,
    wkt,
    within_col,
    weight_col,
    local_max,
    scores,
    mixing,
    entry_rate,
    local_out,
    hdr,
    hdr_all,
    hdr_total,
    hdr_total_all,
    coef_local,
    coef_full,
    entry,
    coef_total,
    mown,
    mrecv,
    usend,
    urecv,
    isend,
    irecv,
    hid,
    send_sem,
    recv_sem,
    relay_sem,
):
    n_seq, n_head = sizes
    n_group = n_seq // MEMBERS
    tok = q_ref.shape[0]
    rows, key_dim = kbuf.shape
    width = vbuf.shape[2]
    value_dim = width * CHUNKS
    part = key_dim // MEMBERS
    seq = lax.axis_index("seq")
    head = lax.axis_index("head")
    me = lax.rem(seq, MEMBERS)
    group = seq // MEMBERS
    base = group * MEMBERS
    head_row = pl.multiple_of(head * tok, tok)

    later = n_group - 1
    K, Q, HDR, GATE = 0, 1, 2, 3
    V, A, C, R = (4 + CHUNKS * i for i in range(4))
    HDRT = 4 + 4 * CHUNKS
    B = HDRT + later

    def member(j):
        return base + lax.rem(me + j, MEMBERS)

    def each_later(act):
        for j in range(1, n_group):
            pl.when(group + j < n_group)(functools.partial(act, j, seq + MEMBERS * j))

    def each_earlier(act):
        for j in range(later):
            pl.when(j < group)(functools.partial(act, j, j * MEMBERS + me))

    def peer(j):
        return lax.rem(head + j, n_head)

    def put(src, dst, which, device, lands=None):
        pltpu.make_async_remote_copy(
            src_ref=src,
            dst_ref=dst,
            send_sem=send_sem.at[which],
            recv_sem=recv_sem.at[which if lands is None else lands],
            device_id=device,
            device_id_type=MESH,
        ).start()

    def arrived(ref, which):
        pltpu.make_async_copy(ref, ref, recv_sem.at[which]).wait()

    def sent(ref, which):
        pltpu.make_async_copy(ref, ref, send_sem.at[which]).wait()

    def local(src, dst, which):
        pltpu.make_async_copy(src, dst, recv_sem.at[which]).start()

    local(ig_ref, gates.at[0], GATE)
    local(fg_ref, gates.at[1], GATE)

    barrier = pltpu.get_barrier_semaphore()
    for j in range(1, n_head):
        pl.semaphore_signal(barrier, inc=1, device_id=(seq, peer(j)), device_id_type=MESH)
    for j in range(1, MEMBERS):
        pl.semaphore_signal(barrier, inc=1, device_id=(member(j), head), device_id_type=MESH)

    def greet(j, there):
        pl.semaphore_signal(barrier, inc=1, device_id=(there, head), device_id_type=MESH)

    each_later(greet)

    def key_cols(h):
        return pl.ds(pl.multiple_of(h * key_dim, key_dim), key_dim)

    def value_cols(h, c):
        return pl.ds(pl.multiple_of(h * value_dim + c * width, width), width)

    my_rows = pl.ds(head_row, tok)
    local(k_ref.at[:, key_cols(head)], kbuf.at[my_rows], K)
    for c in range(CHUNKS):
        local(v_ref.at[:, value_cols(head, c)], vbuf.at[c, my_rows], V + c)
    local(q_ref.at[:, key_cols(head)], qbuf.at[my_rows], Q)

    arrived(gates, GATE)
    gate = gates[0]
    forget = gates[1]
    log_keep = jnp.minimum(forget, 0.0) - jnp.log1p(jnp.exp(-jnp.abs(forget)))
    lane = lax.broadcasted_iota(jnp.int32, (8, rows), 1)
    within_row = jnp.broadcast_to(log_keep, (8, rows))
    step = 1
    while step < rows:
        within_row = within_row + jnp.where(lane >= step, pltpu.roll(within_row, step, 1), 0.0)
        step *= 2
    within_row = within_row[0:1, :]
    decay = within_row[:, rows - 1 : rows]
    gate_less = gate - within_row

    def gate_tile(i, peak):
        at = pl.ds(pl.multiple_of(i * TILE, TILE), TILE)
        t = lax.broadcasted_iota(jnp.int32, (TILE, rows), 0) + i * TILE
        s = lax.broadcasted_iota(jnp.int32, (TILE, rows), 1)
        col = jnp.sum(jnp.where(s <= t, log_keep, 0.0), axis=1, keepdims=True)
        own_gate = jnp.sum(jnp.where(s == t, gate, 0.0), axis=1, keepdims=True)
        since = decay - col + own_gate
        within_col[at, :] = col
        weight_col[at, :] = since
        local_max[at, :] = col + jnp.max(
            jnp.where(s <= t, gate_less, NEG_FILL), axis=1, keepdims=True
        )
        return jnp.maximum(peak, jnp.max(since, axis=0, keepdims=True))

    peak_own = lax.fori_loop(
        0, rows // TILE, gate_tile, jnp.full((1, 1), -jnp.inf, jnp.float32)
    )
    hdr[...] = jnp.zeros_like(hdr)
    hdr[0:1, :] = jnp.broadcast_to(decay, (1, 128))
    hdr[1:2, :] = jnp.broadcast_to(peak_own, (1, 128))
    hdr_total[...] = jnp.zeros_like(hdr_total)
    for j in range(later):

        @pl.when(j >= group)
        def _():
            hdr_total_all[j] = jnp.zeros(hdr_total.shape, jnp.float32)
            for c in range(CHUNKS):
                urecv[c, j] = jnp.zeros(urecv.shape[2:], urecv.dtype)

    pl.semaphore_wait(barrier, n_head - 1 + MEMBERS - 1 + group)

    def answer(j, there):
        pl.semaphore_signal(relay_sem, inc=1, device_id=(there, head), device_id_type=MESH)

    each_earlier(answer)

    for j in range(1, n_head):
        h = peer(j)
        put(k_ref.at[:, key_cols(h)], kbuf.at[my_rows], K, (seq, h))
    for c in range(CHUNKS):
        for j in range(1, n_head):
            h = peer(j)
            put(v_ref.at[:, value_cols(h, c)], vbuf.at[c, my_rows], V + c, (seq, h))
    for j in range(1, n_head):
        h = peer(j)
        put(q_ref.at[:, key_cols(h)], qbuf.at[my_rows], Q, (seq, h))

    arrived(kbuf, K)

    def key_tile(i, normal):
        at = pl.ds(pl.multiple_of(i * TILE, TILE), TILE)
        weight = jnp.exp(weight_col[at, :] - peak_own)
        weighted = weight * kbuf[at, :].astype(jnp.float32)
        wkt[:, at] = weighted.T.astype(jnp.bfloat16)
        return normal + jnp.sum(weighted, axis=0, keepdims=True)

    normal_own = lax.fori_loop(
        0, rows // TILE, key_tile, jnp.zeros((1, key_dim), jnp.float32)
    )
    for i in range(key_dim // 128):
        hdr[2 + i : 3 + i, :] = normal_own[:, i * 128 : (i + 1) * 128]
    hdr_all[me] = hdr[...]
    for j in range(1, MEMBERS):
        put(hdr, hdr_all.at[me], HDR, (member(j), head))

    for c in range(CHUNKS):
        arrived(vbuf.at[c], V + c)
        own = jnp.dot(wkt[...], vbuf[c], preferred_element_type=jnp.float32)
        mown[c] = own.astype(jnp.bfloat16).reshape(MEMBERS, part, width)
        for j in range(1, MEMBERS):
            g = lax.rem(me + j, MEMBERS)
            put(mown.at[c, g], mrecv.at[c, me], A + c, (base + g, head))
        mrecv[c, me] = mown[c, me]

    norm_rows = slice(2, 2 + key_dim // 128)
    no_peak = jnp.full((1, 128), NEG_FILL, jnp.float32)
    no_norm = jnp.zeros((key_dim // 128, 128), jnp.float32)

    arrived(hdr_all.at[pl.ds(0, MEMBERS - 1)], HDR)
    peak, norm, total = no_peak, no_norm, jnp.zeros((1, 128), jnp.float32)
    for g in range(MEMBERS):
        d, p = hdr_all[g, 0:1, :], hdr_all[g, 1:2, :]
        new = jnp.maximum(d + peak, p)
        older, newer = jnp.exp(d + peak - new), jnp.exp(p - new)
        coef_local[g, 0:1, :] = older
        coef_local[g, 1:2, :] = newer
        norm = older * norm + newer * hdr_all[g, norm_rows, :]
        peak, total = new, total + d
    hdr_total[0:1, :] = total
    hdr_total[1:2, :] = peak
    hdr_total[norm_rows, :] = norm

    @pl.when(group < later)
    def _():
        pl.semaphore_wait(relay_sem, later - group)

    def send_header(j, there):
        put(hdr_total, hdr_total_all.at[group], HDRT + j - 1, (there, head), HDRT + group)

    each_later(send_header)

    arrived(qbuf, Q)
    scale = key_dim ** (-0.5)

    def score_tile(i, carry):
        at = pl.ds(pl.multiple_of(i * TILE, TILE), TILE)
        scores[at, :] = lax.dot_general(
            qbuf[at, :], kbuf[...], (((1,), (1,)), ((), ())), preferred_element_type=jnp.float32
        )
        return carry

    lax.fori_loop(0, rows // TILE, score_tile, 0)

    def wide(row):
        return jnp.concatenate([row] * (width // 128), axis=1)

    for c in range(CHUNKS):
        arrived(mrecv.at[c, pl.ds(0, MEMBERS - 1)], A + c)
        state = jnp.zeros((part, width), jnp.float32)
        for g in range(MEMBERS):
            state = (
                wide(coef_local[g, 0:1, :]) * state
                + wide(coef_local[g, 1:2, :]) * mrecv[c, g].astype(jnp.float32)
            )
        usend[c] = state.astype(jnp.bfloat16)

        def send_total(j, there):
            at = B + later * c
            put(usend.at[c], urecv.at[c, group], at + j - 1, (there, head), at + group)

        each_later(send_total)

    each_earlier(lambda j, there: arrived(hdr_total_all.at[j], HDRT + j))
    peak, norm = no_peak, no_norm
    for j in range(n_group - 1):
        d, p = hdr_total_all[j, 0:1, :], hdr_total_all[j, 1:2, :]
        new = jnp.maximum(d + peak, p)
        used = j < group
        older = jnp.where(used, jnp.exp(d + peak - new), 1.0)
        newer = jnp.where(used, jnp.exp(p - new), 0.0)
        coef_total[j, 0:1, :] = older
        coef_total[j, 1:2, :] = newer
        norm = jnp.where(used, older * norm + newer * hdr_total_all[j, norm_rows, :], norm)
        peak = jnp.where(used, new, peak)
    for g in range(MEMBERS):
        entry[g, 1:2, :] = peak
        entry[g, norm_rows, :] = norm
        d, p = hdr_all[g, 0:1, :], hdr_all[g, 1:2, :]
        new = jnp.maximum(d + peak, p)
        older, newer = jnp.exp(d + peak - new), jnp.exp(p - new)
        coef_full[g, 0:1, :] = older
        coef_full[g, 1:2, :] = newer
        norm = older * norm + newer * hdr_all[g, norm_rows, :]
        peak = new

    my_entry = entry[me]
    peak_in = my_entry[1:2, 0:1]
    normal_in = jnp.concatenate(
        [my_entry[2 + i : 3 + i, :] for i in range(key_dim // 128)], axis=1
    )

    def mixing_tile(i, carry):
        at = pl.ds(pl.multiple_of(i * TILE, TILE), TILE)
        t = lax.broadcasted_iota(jnp.int32, (TILE, rows), 0) + i * TILE
        s = lax.broadcasted_iota(jnp.int32, (TILE, rows), 1)
        col = within_col[at, :]
        entry_log = col + peak_in
        peak_row = jnp.maximum(entry_log, local_max[at, :])
        logs = jnp.where(s <= t, (col - peak_row) + gate_less, NEG_FILL)
        mix = jnp.exp(logs) * (scores[at, :] * scale)
        mixing[at, :] = mix.astype(jnp.bfloat16)
        rate = jnp.exp(entry_log - peak_row)
        from_normal = jnp.sum(
            qbuf[at, :].astype(jnp.float32) * normal_in, axis=1, keepdims=True
        )
        below = jnp.sum(mix, axis=1, keepdims=True) + rate * (from_normal * scale)
        inverse = 1.0 / jnp.maximum(jnp.abs(below), 1.0)
        entry_rate[at, 0:1] = rate * inverse * scale
        entry_rate[at, 1:2] = inverse
        return carry

    lax.fori_loop(0, rows // TILE, mixing_tile, 0)

    for c in range(CHUNKS):
        each_earlier(lambda j, there: arrived(urecv.at[c, j], B + later * c + j))
        state = jnp.zeros((part, width), jnp.float32)
        for j in range(n_group - 1):
            state = jnp.where(
                j < group,
                wide(coef_total[j, 0:1, :]) * state
                + wide(coef_total[j, 1:2, :]) * urecv[c, j].astype(jnp.float32),
                state,
            )
        for g in range(MEMBERS):
            isend[c, g] = state.astype(jnp.bfloat16)
            state = (
                wide(coef_full[g, 0:1, :]) * state
                + wide(coef_full[g, 1:2, :]) * mrecv[c, g].astype(jnp.float32)
            )
        my_part = pl.ds(pl.multiple_of(me * part, part), part)
        for j in range(1, MEMBERS):
            g = lax.rem(me + j, MEMBERS)
            put(isend.at[c, g], irecv.at[c, my_part], C + c, (base + g, head))
        irecv[c, my_part] = isend[c, me]

    def local_tile(i, carry):
        at = pl.ds(pl.multiple_of(i * TILE, TILE), TILE)
        for c in range(CHUNKS):
            local_out[c, at, :] = entry_rate[at, 1:2] * jnp.dot(
                mixing[at, :], vbuf[c], preferred_element_type=jnp.float32
            )
        return carry

    lax.fori_loop(0, rows // TILE, local_tile, 0)

    for c in range(CHUNKS):
        arrived(irecv.at[c, pl.ds(0, key_dim - part)], C + c)

        def out_tile(i, carry):
            at = pl.ds(pl.multiple_of(i * TILE, TILE), TILE)
            from_memory = jnp.dot(
                qbuf[at, :], irecv[c], preferred_element_type=jnp.float32
            )
            hid[c, at, :] = (
                local_out[c, at, :] + entry_rate[at, 0:1] * from_memory
            ).astype(jnp.bfloat16)
            return carry

        lax.fori_loop(0, rows // TILE, out_tile, 0)
        for j in range(1, n_head):
            h = peer(j)
            put(
                hid.at[c, pl.ds(pl.multiple_of(h * tok, tok), tok)],
                ret_ref.at[:, value_cols(head, c)],
                R + c,
                (seq, h),
            )
        local(hid.at[c, my_rows], ret_ref.at[:, value_cols(head, c)], R + c)

    for c in range(CHUNKS):
        arrived(hid.at[c], R + c)

    peers_rows = pl.ds(0, rows - tok)
    sent(kbuf.at[peers_rows], K)
    sent(qbuf.at[peers_rows], Q)
    sent(hdr_all.at[pl.ds(0, MEMBERS - 1)], HDR)
    each_later(lambda j, there: sent(hdr_total, HDRT + j - 1))
    for c in range(CHUNKS):
        sent(vbuf.at[c, peers_rows], V + c)
        sent(mrecv.at[c, pl.ds(0, MEMBERS - 1)], A + c)
        each_later(lambda j, there: sent(usend.at[c], B + later * c + j - 1))
        sent(irecv.at[c, pl.ds(0, key_dim - part)], C + c)
        sent(hid.at[c, peers_rows], R + c)


def per_device(n_seq, n_head, queries, keys, values, in_gate, forget_gate, out_gate):
    tok = queries.shape[0]
    rows = tok * n_head
    key_dim = queries.shape[1] // n_head
    value_dim = values.shape[1] // n_head
    width = value_dim // CHUNKS
    part = key_dim // MEMBERS
    n_group = n_seq // MEMBERS
    bf16, f32 = jnp.bfloat16, jnp.float32
    n_sem = 4 + 4 * CHUNKS + (n_group - 1) * (1 + CHUNKS)
    scratch = [
        pltpu.VMEM((2, 1, rows), f32),
        pltpu.VMEM((rows, key_dim), bf16),
        pltpu.VMEM((rows, key_dim), bf16),
        pltpu.VMEM((CHUNKS, rows, width), bf16),
        pltpu.VMEM((key_dim, rows), bf16),
        pltpu.VMEM((rows, 1), f32),
        pltpu.VMEM((rows, 1), f32),
        pltpu.VMEM((rows, 1), f32),
        pltpu.VMEM((rows, rows), f32),
        pltpu.VMEM((rows, rows), bf16),
        pltpu.VMEM((rows, 2), f32),
        pltpu.VMEM((CHUNKS, rows, width), f32),
        pltpu.VMEM((8, 128), f32),
        pltpu.VMEM((MEMBERS, 8, 128), f32),
        pltpu.VMEM((8, 128), f32),
        pltpu.VMEM((n_group, 8, 128), f32),
        pltpu.VMEM((MEMBERS, 8, 128), f32),
        pltpu.VMEM((MEMBERS, 8, 128), f32),
        pltpu.VMEM((MEMBERS, 8, 128), f32),
        pltpu.VMEM((n_group, 8, 128), f32),
        pltpu.VMEM((CHUNKS, MEMBERS, part, width), bf16),
        pltpu.VMEM((CHUNKS, MEMBERS, part, width), bf16),
        pltpu.VMEM((CHUNKS, part, width), bf16),
        pltpu.VMEM((CHUNKS, n_group, part, width), bf16),
        pltpu.VMEM((CHUNKS, MEMBERS, part, width), bf16),
        pltpu.VMEM((CHUNKS, key_dim, width), bf16),
        pltpu.VMEM((CHUNKS, rows, width), bf16),
        pltpu.SemaphoreType.DMA((n_sem,)),
        pltpu.SemaphoreType.DMA((n_sem,)),
        pltpu.SemaphoreType.REGULAR,
    ]
    anywhere = pl.BlockSpec(memory_space=pl.ANY)
    hbm = pl.BlockSpec(memory_space=pltpu.HBM)
    returned = pl.pallas_call(
        functools.partial(kernel, (n_seq, n_head)),
        out_shape=pltpu.VMEM((tok, n_head * value_dim), bf16),
        in_specs=[hbm] * 5,
        out_specs=pl.BlockSpec(memory_space=pltpu.VMEM),
        scratch_shapes=scratch,
        compiler_params=pltpu.CompilerParams(
            collective_id=0, has_side_effects=True, vmem_limit_bytes=60 * 2**20
        ),
    )(queries, keys, values, in_gate, forget_gate)
    gated = jax.nn.sigmoid(out_gate.astype(f32)) * returned.astype(f32)
    return gated.astype(bf16)


def solution(mesh):
    return jax.shard_map(
        functools.partial(per_device, mesh.shape["seq"], mesh.shape["head"]),
        mesh=mesh,
        in_specs=(
            P(("seq", "head"), None),
            P(("seq", "head"), None),
            P(("seq", "head"), None),
            P("head", "seq"),
            P("head", "seq"),
            P(("seq", "head"), None),
        ),
        out_specs=P(("seq", "head"), None),
        check_vma=False,
    )
```

```python
import functools

import jax
import jax.numpy as jnp
from jax import lax
from jax.experimental import pallas as pl
from jax.experimental.pallas import tpu as pltpu
from jax.sharding import PartitionSpec as P

MESH = pl.DeviceIdType.MESH
NEG_FILL = -1e30
MEMBERS = 16
CHUNKS = 4
TILE = 128
PEERS = ((2, 0), (1, 0), (3, 0), (2, 1), (1, 1), (3, 1), (0, 1))


def kernel(
    sizes,
    q_ref,
    k_ref,
    v_ref,
    ig_ref,
    fg_ref,
    ret_ref,
    gates,
    qbuf,
    kbuf,
    vbuf,
    wkt,
    within_col,
    weight_col,
    local_max,
    scores,
    mixing,
    entry_rate,
    local_out,
    hdr,
    hdr_all,
    hdr_total,
    hdr_total_all,
    coef_local,
    coef_full,
    entry,
    coef_total,
    mown,
    mrecv,
    usend,
    urecv,
    isend,
    irecv,
    hid,
    send_sem,
    recv_sem,
    relay_sem,
):
    n_seq, n_head = sizes
    n_group = n_seq // MEMBERS
    tok = q_ref.shape[0]
    rows, key_dim = kbuf.shape
    width = vbuf.shape[2]
    value_dim = width * CHUNKS
    part = key_dim // MEMBERS
    seq = lax.axis_index("seq")
    head = lax.axis_index("head")
    me = lax.rem(seq, MEMBERS)
    group = seq // MEMBERS
    base = group * MEMBERS
    head_row = pl.multiple_of(head * tok, tok)

    later = n_group - 1
    K, Q, HDR, GATE = 0, 1, 2, 3
    V, A, C, R = (4 + CHUNKS * i for i in range(4))
    HDRT = 4 + 4 * CHUNKS
    B = HDRT + later

    def member(j):
        return base + lax.rem(me + j, MEMBERS)

    def each_later(act):
        for j in (2, 3, 1):
            pl.when(group + j < n_group)(functools.partial(act, j, seq + MEMBERS * j))

    def each_earlier(act):
        for j in range(later):
            pl.when(j < group)(functools.partial(act, j, j * MEMBERS + me))

    def peer(j):
        chip, flip = PEERS[j - 1]
        core = lax.rem(head, 2)
        there = lax.rem(head // 2 + chip, n_head // 2)
        return 2 * there + (1 - core if flip else core)

    def put(src, dst, which, device, lands=None):
        pltpu.make_async_remote_copy(
            src_ref=src,
            dst_ref=dst,
            send_sem=send_sem.at[which],
            recv_sem=recv_sem.at[which if lands is None else lands],
            device_id=device,
            device_id_type=MESH,
        ).start()

    def arrived(ref, which):
        pltpu.make_async_copy(ref, ref, recv_sem.at[which]).wait()

    def sent(ref, which):
        pltpu.make_async_copy(ref, ref, send_sem.at[which]).wait()

    def local(src, dst, which):
        pltpu.make_async_copy(src, dst, recv_sem.at[which]).start()

    local(ig_ref, gates.at[0], GATE)
    local(fg_ref, gates.at[1], GATE)

    barrier = pltpu.get_barrier_semaphore()
    for j in range(1, n_head):
        pl.semaphore_signal(barrier, inc=1, device_id=(seq, peer(j)), device_id_type=MESH)
    for j in range(1, MEMBERS):
        pl.semaphore_signal(barrier, inc=1, device_id=(member(j), head), device_id_type=MESH)

    def greet(j, there):
        pl.semaphore_signal(barrier, inc=1, device_id=(there, head), device_id_type=MESH)

    each_later(greet)

    def key_cols(h):
        return pl.ds(pl.multiple_of(h * key_dim, key_dim), key_dim)

    def value_cols(h, c):
        return pl.ds(pl.multiple_of(h * value_dim + c * width, width), width)

    my_rows = pl.ds(head_row, tok)
    local(k_ref.at[:, key_cols(head)], kbuf.at[my_rows], K)
    for c in range(CHUNKS):
        local(v_ref.at[:, value_cols(head, c)], vbuf.at[c, my_rows], V + c)
    local(q_ref.at[:, key_cols(head)], qbuf.at[my_rows], Q)

    for j in range(later):

        @pl.when(j >= group)
        def _():
            hdr_total_all[j] = jnp.zeros(hdr_total.shape, jnp.float32)
            for c in range(CHUNKS):
                urecv[c, j] = jnp.zeros(urecv.shape[2:], urecv.dtype)

    pl.semaphore_wait(barrier, n_head - 1 + MEMBERS - 1 + group)

    def answer(j, there):
        pl.semaphore_signal(relay_sem, inc=1, device_id=(there, head), device_id_type=MESH)

    each_earlier(answer)

    for j in range(1, n_head):
        h = peer(j)
        put(k_ref.at[:, key_cols(h)], kbuf.at[my_rows], K, (seq, h))
    for c in range(CHUNKS):
        for j in range(1, n_head):
            h = peer(j)
            put(v_ref.at[:, value_cols(h, c)], vbuf.at[c, my_rows], V + c, (seq, h))
    for j in range(1, n_head):
        h = peer(j)
        put(q_ref.at[:, key_cols(h)], qbuf.at[my_rows], Q, (seq, h))

    arrived(gates, GATE)
    gate = gates[0]
    forget = gates[1]
    log_keep = jnp.minimum(forget, 0.0) - jnp.log1p(jnp.exp(-jnp.abs(forget)))
    lane = lax.broadcasted_iota(jnp.int32, (8, rows), 1)
    within_row = jnp.broadcast_to(log_keep, (8, rows))
    step = 1
    while step < rows:
        within_row = within_row + jnp.where(lane >= step, pltpu.roll(within_row, step, 1), 0.0)
        step *= 2
    within_row = within_row[0:1, :]
    decay = within_row[:, rows - 1 : rows]
    gate_less = gate - within_row

    def gate_tile(i, peak):
        at = pl.ds(pl.multiple_of(i * TILE, TILE), TILE)
        t = lax.broadcasted_iota(jnp.int32, (TILE, rows), 0) + i * TILE
        s = lax.broadcasted_iota(jnp.int32, (TILE, rows), 1)
        col = jnp.sum(jnp.where(s <= t, log_keep, 0.0), axis=1, keepdims=True)
        own_gate = jnp.sum(jnp.where(s == t, gate, 0.0), axis=1, keepdims=True)
        since = decay - col + own_gate
        within_col[at, :] = col
        weight_col[at, :] = since
        local_max[at, :] = col + jnp.max(
            jnp.where(s <= t, gate_less, NEG_FILL), axis=1, keepdims=True
        )
        return jnp.maximum(peak, jnp.max(since, axis=0, keepdims=True))

    peak_own = lax.fori_loop(
        0, rows // TILE, gate_tile, jnp.full((1, 1), -jnp.inf, jnp.float32)
    )
    hdr[...] = jnp.zeros_like(hdr)
    hdr[0:1, :] = jnp.broadcast_to(decay, (1, 128))
    hdr[1:2, :] = jnp.broadcast_to(peak_own, (1, 128))
    hdr_total[...] = jnp.zeros_like(hdr_total)
    arrived(kbuf, K)

    def key_tile(i, normal):
        at = pl.ds(pl.multiple_of(i * TILE, TILE), TILE)
        weight = jnp.exp(weight_col[at, :] - peak_own)
        weighted = weight * kbuf[at, :].astype(jnp.float32)
        wkt[:, at] = weighted.T.astype(jnp.bfloat16)
        return normal + jnp.sum(weighted, axis=0, keepdims=True)

    normal_own = lax.fori_loop(
        0, rows // TILE, key_tile, jnp.zeros((1, key_dim), jnp.float32)
    )
    for i in range(key_dim // 128):
        hdr[2 + i : 3 + i, :] = normal_own[:, i * 128 : (i + 1) * 128]
    hdr_all[me] = hdr[...]
    for j in range(1, MEMBERS):
        put(hdr, hdr_all.at[me], HDR, (member(j), head))

    for c in range(CHUNKS):
        arrived(vbuf.at[c], V + c)
        own = jnp.dot(wkt[...], vbuf[c], preferred_element_type=jnp.float32)
        mown[c] = own.astype(jnp.bfloat16).reshape(MEMBERS, part, width)
        for j in range(1, MEMBERS):
            g = lax.rem(me + j, MEMBERS)
            put(mown.at[c, g], mrecv.at[c, me], A + c, (base + g, head))
        mrecv[c, me] = mown[c, me]

    norm_rows = slice(2, 2 + key_dim // 128)
    no_peak = jnp.full((1, 128), NEG_FILL, jnp.float32)
    no_norm = jnp.zeros((key_dim // 128, 128), jnp.float32)

    arrived(hdr_all.at[pl.ds(0, MEMBERS - 1)], HDR)
    peak, norm, total = no_peak, no_norm, jnp.zeros((1, 128), jnp.float32)
    for g in range(MEMBERS):
        d, p = hdr_all[g, 0:1, :], hdr_all[g, 1:2, :]
        new = jnp.maximum(d + peak, p)
        older, newer = jnp.exp(d + peak - new), jnp.exp(p - new)
        coef_local[g, 0:1, :] = older
        coef_local[g, 1:2, :] = newer
        norm = older * norm + newer * hdr_all[g, norm_rows, :]
        peak, total = new, total + d
    hdr_total[0:1, :] = total
    hdr_total[1:2, :] = peak
    hdr_total[norm_rows, :] = norm

    @pl.when(group < later)
    def _():
        pl.semaphore_wait(relay_sem, later - group)

    def send_header(j, there):
        put(hdr_total, hdr_total_all.at[group], HDRT + j - 1, (there, head), HDRT + group)

    each_later(send_header)

    arrived(qbuf, Q)
    scale = key_dim ** (-0.5)

    def score_tile(i, carry):
        at = pl.ds(pl.multiple_of(i * TILE, TILE), TILE)
        scores[at, :] = lax.dot_general(
            qbuf[at, :], kbuf[...], (((1,), (1,)), ((), ())), preferred_element_type=jnp.float32
        )
        return carry

    lax.fori_loop(0, rows // TILE, score_tile, 0)

    def wide(row):
        return jnp.concatenate([row] * (width // 128), axis=1)

    for c in range(CHUNKS):
        arrived(mrecv.at[c, pl.ds(0, MEMBERS - 1)], A + c)
        state = jnp.zeros((part, width), jnp.float32)
        for g in range(MEMBERS):
            state = (
                wide(coef_local[g, 0:1, :]) * state
                + wide(coef_local[g, 1:2, :]) * mrecv[c, g].astype(jnp.float32)
            )
        usend[c] = state.astype(jnp.bfloat16)

        def send_total(j, there):
            at = B + later * c
            put(usend.at[c], urecv.at[c, group], at + j - 1, (there, head), at + group)

        each_later(send_total)

    each_earlier(lambda j, there: arrived(hdr_total_all.at[j], HDRT + j))
    peak, norm = no_peak, no_norm
    for j in range(n_group - 1):
        d, p = hdr_total_all[j, 0:1, :], hdr_total_all[j, 1:2, :]
        new = jnp.maximum(d + peak, p)
        used = j < group
        older = jnp.where(used, jnp.exp(d + peak - new), 1.0)
        newer = jnp.where(used, jnp.exp(p - new), 0.0)
        coef_total[j, 0:1, :] = older
        coef_total[j, 1:2, :] = newer
        norm = jnp.where(used, older * norm + newer * hdr_total_all[j, norm_rows, :], norm)
        peak = jnp.where(used, new, peak)
    for g in range(MEMBERS):
        entry[g, 1:2, :] = peak
        entry[g, norm_rows, :] = norm
        d, p = hdr_all[g, 0:1, :], hdr_all[g, 1:2, :]
        new = jnp.maximum(d + peak, p)
        older, newer = jnp.exp(d + peak - new), jnp.exp(p - new)
        coef_full[g, 0:1, :] = older
        coef_full[g, 1:2, :] = newer
        norm = older * norm + newer * hdr_all[g, norm_rows, :]
        peak = new

    for c in range(CHUNKS):
        each_earlier(lambda j, there: arrived(urecv.at[c, j], B + later * c + j))
        state = jnp.zeros((part, width), jnp.float32)
        for j in range(n_group - 1):
            state = jnp.where(
                j < group,
                wide(coef_total[j, 0:1, :]) * state
                + wide(coef_total[j, 1:2, :]) * urecv[c, j].astype(jnp.float32),
                state,
            )
        for g in range(MEMBERS):
            isend[c, g] = state.astype(jnp.bfloat16)
            state = (
                wide(coef_full[g, 0:1, :]) * state
                + wide(coef_full[g, 1:2, :]) * mrecv[c, g].astype(jnp.float32)
            )
        my_part = pl.ds(pl.multiple_of(me * part, part), part)
        for j in range(1, MEMBERS):
            g = lax.rem(me + j, MEMBERS)
            put(isend.at[c, g], irecv.at[c, my_part], C + c, (base + g, head))
        irecv[c, my_part] = isend[c, me]

    my_entry = entry[me]
    peak_in = my_entry[1:2, 0:1]
    normal_in = jnp.concatenate(
        [my_entry[2 + i : 3 + i, :] for i in range(key_dim // 128)], axis=1
    )

    def mixing_tile(i, carry):
        at = pl.ds(pl.multiple_of(i * TILE, TILE), TILE)
        t = lax.broadcasted_iota(jnp.int32, (TILE, rows), 0) + i * TILE
        s = lax.broadcasted_iota(jnp.int32, (TILE, rows), 1)
        col = within_col[at, :]
        entry_log = col + peak_in
        peak_row = jnp.maximum(entry_log, local_max[at, :])
        logs = jnp.where(s <= t, (col - peak_row) + gate_less, NEG_FILL)
        mix = jnp.exp(logs) * (scores[at, :] * scale)
        mixing[at, :] = mix.astype(jnp.bfloat16)
        rate = jnp.exp(entry_log - peak_row)
        from_normal = jnp.sum(
            qbuf[at, :].astype(jnp.float32) * normal_in, axis=1, keepdims=True
        )
        below = jnp.sum(mix, axis=1, keepdims=True) + rate * (from_normal * scale)
        inverse = 1.0 / jnp.maximum(jnp.abs(below), 1.0)
        entry_rate[at, 0:1] = rate * inverse * scale
        entry_rate[at, 1:2] = inverse
        return carry

    lax.fori_loop(0, rows // TILE, mixing_tile, 0)

    def local_tile(i, carry):
        at = pl.ds(pl.multiple_of(i * TILE, TILE), TILE)
        for c in range(CHUNKS):
            local_out[c, at, :] = entry_rate[at, 1:2] * jnp.dot(
                mixing[at, :], vbuf[c], preferred_element_type=jnp.float32
            )
        return carry

    lax.fori_loop(0, rows // TILE, local_tile, 0)

    def send_hidden(c, h):
        put(
            hid.at[c, pl.ds(pl.multiple_of(h * tok, tok), tok)],
            ret_ref.at[:, value_cols(head, c)],
            R + c,
            (seq, h),
        )

    for c in range(CHUNKS):
        arrived(irecv.at[c, pl.ds(0, key_dim - part)], C + c)

        for i in range(n_head // 2 - 1, -1, -1):
            chip = lax.rem(head // 2 + (i + 1) % (n_head // 2), n_head // 2)
            at = pl.ds(pl.multiple_of(chip * 2 * tok, 2 * tok), 2 * tok)
            from_memory = jnp.dot(
                qbuf[at, :], irecv[c], preferred_element_type=jnp.float32
            )
            hid[c, at, :] = (
                local_out[c, at, :] + entry_rate[at, 0:1] * from_memory
            ).astype(jnp.bfloat16)
            for core in range(2):
                h = 2 * chip + core
                pl.when(h != head)(functools.partial(send_hidden, c, h))
        local(hid.at[c, my_rows], ret_ref.at[:, value_cols(head, c)], R + c)

    for c in range(CHUNKS):
        arrived(hid.at[c], R + c)

    peers_rows = pl.ds(0, rows - tok)
    sent(kbuf.at[peers_rows], K)
    sent(qbuf.at[peers_rows], Q)
    sent(hdr_all.at[pl.ds(0, MEMBERS - 1)], HDR)
    each_later(lambda j, there: sent(hdr_total, HDRT + j - 1))
    for c in range(CHUNKS):
        sent(vbuf.at[c, peers_rows], V + c)
        sent(mrecv.at[c, pl.ds(0, MEMBERS - 1)], A + c)
        each_later(lambda j, there: sent(usend.at[c], B + later * c + j - 1))
        sent(irecv.at[c, pl.ds(0, key_dim - part)], C + c)
        sent(hid.at[c, peers_rows], R + c)


def per_device(n_seq, n_head, queries, keys, values, in_gate, forget_gate, out_gate):
    tok = queries.shape[0]
    rows = tok * n_head
    key_dim = queries.shape[1] // n_head
    value_dim = values.shape[1] // n_head
    width = value_dim // CHUNKS
    part = key_dim // MEMBERS
    n_group = n_seq // MEMBERS
    bf16, f32 = jnp.bfloat16, jnp.float32
    n_sem = 4 + 4 * CHUNKS + (n_group - 1) * (1 + CHUNKS)
    scratch = [
        pltpu.VMEM((2, 1, rows), f32),
        pltpu.VMEM((rows, key_dim), bf16),
        pltpu.VMEM((rows, key_dim), bf16),
        pltpu.VMEM((CHUNKS, rows, width), bf16),
        pltpu.VMEM((key_dim, rows), bf16),
        pltpu.VMEM((rows, 1), f32),
        pltpu.VMEM((rows, 1), f32),
        pltpu.VMEM((rows, 1), f32),
        pltpu.VMEM((rows, rows), f32),
        pltpu.VMEM((rows, rows), bf16),
        pltpu.VMEM((rows, 2), f32),
        pltpu.VMEM((CHUNKS, rows, width), f32),
        pltpu.VMEM((8, 128), f32),
        pltpu.VMEM((MEMBERS, 8, 128), f32),
        pltpu.VMEM((8, 128), f32),
        pltpu.VMEM((n_group, 8, 128), f32),
        pltpu.VMEM((MEMBERS, 8, 128), f32),
        pltpu.VMEM((MEMBERS, 8, 128), f32),
        pltpu.VMEM((MEMBERS, 8, 128), f32),
        pltpu.VMEM((n_group, 8, 128), f32),
        pltpu.VMEM((CHUNKS, MEMBERS, part, width), bf16),
        pltpu.VMEM((CHUNKS, MEMBERS, part, width), bf16),
        pltpu.VMEM((CHUNKS, part, width), bf16),
        pltpu.VMEM((CHUNKS, n_group, part, width), bf16),
        pltpu.VMEM((CHUNKS, MEMBERS, part, width), bf16),
        pltpu.VMEM((CHUNKS, key_dim, width), bf16),
        pltpu.VMEM((CHUNKS, rows, width), bf16),
        pltpu.SemaphoreType.DMA((n_sem,)),
        pltpu.SemaphoreType.DMA((n_sem,)),
        pltpu.SemaphoreType.REGULAR,
    ]
    anywhere = pl.BlockSpec(memory_space=pl.ANY)
    hbm = pl.BlockSpec(memory_space=pltpu.HBM)
    returned = pl.pallas_call(
        functools.partial(kernel, (n_seq, n_head)),
        out_shape=pltpu.VMEM((tok, n_head * value_dim), bf16),
        in_specs=[hbm] * 5,
        out_specs=pl.BlockSpec(memory_space=pltpu.VMEM),
        scratch_shapes=scratch,
        compiler_params=pltpu.CompilerParams(
            collective_id=0, has_side_effects=True, vmem_limit_bytes=60 * 2**20
        ),
    )(queries, keys, values, in_gate, forget_gate)
    gated = jax.nn.sigmoid(out_gate.astype(f32)) * returned.astype(f32)
    return gated.astype(bf16)


def solution(mesh):
    return jax.shard_map(
        functools.partial(per_device, mesh.shape["seq"], mesh.shape["head"]),
        mesh=mesh,
        in_specs=(
            P(("seq", "head"), None),
            P(("seq", "head"), None),
            P(("seq", "head"), None),
            P("head", "seq"),
            P("head", "seq"),
            P(("seq", "head"), None),
        ),
        out_specs=P(("seq", "head"), None),
        check_vma=False,
    )
```

```python
import functools

import jax
import jax.numpy as jnp
from jax import lax
from jax.experimental import pallas as pl
from jax.experimental.pallas import tpu as pltpu
from jax.sharding import PartitionSpec as P

MESH = pl.DeviceIdType.MESH
NEG_FILL = -1e30
MEMBERS = 16
CHUNKS = 4
TILE = 128
LAG = 1
PEERS = ((2, 0), (1, 0), (3, 0), (2, 1), (1, 1), (3, 1), (0, 1))


def kernel(
    sizes,
    q_ref,
    k_ref,
    v_ref,
    ig_ref,
    fg_ref,
    ret_ref,
    gates,
    qbuf,
    kbuf,
    vbuf,
    wkt,
    within_col,
    weight_col,
    local_max,
    scores,
    mixing,
    entry_rate,
    local_out,
    hdr,
    hdr_all,
    nrm,
    nrm_all,
    hdr_total,
    hdr_total_all,
    coef_local,
    coef_full,
    entry,
    coef_total,
    mown,
    mrecv,
    usend,
    umerged,
    urecv,
    isend,
    irecv,
    hid,
    send_sem,
    recv_sem,
    relay_sem,
):
    n_seq, n_head = sizes
    n_group = n_seq // MEMBERS
    tok = q_ref.shape[0]
    rows, key_dim = kbuf.shape
    width = vbuf.shape[2]
    value_dim = width * CHUNKS
    part = key_dim // MEMBERS
    seq = lax.axis_index("seq")
    head = lax.axis_index("head")
    me = lax.rem(seq, MEMBERS)
    group = seq // MEMBERS
    base = group * MEMBERS
    head_row = pl.multiple_of(head * tok, tok)

    later = n_group - 1
    K, Q, HDR, NRM, GATE = range(5)
    V, A, C, R = (5 + CHUNKS * i for i in range(4))
    HDRT = 5 + 4 * CHUNKS
    B = HDRT + later

    turned = jnp.where(group == later, MEMBERS // 2, 0)
    mine = lax.rem(me + turned, MEMBERS)

    def member(j):
        return base + lax.rem(me + j, MEMBERS)

    def owner_later(j):
        turn = jnp.where(group + j == later, MEMBERS // 2, 0)
        return (group + j) * MEMBERS + lax.rem(me + turn, MEMBERS)

    def each_later(act):
        for j in (2, 3, 1):
            pl.when(group + j < n_group)(functools.partial(act, j, owner_later(j)))

    def each_earlier(act):
        for j in range(later):
            pl.when(j < group)(functools.partial(act, j, j * MEMBERS + mine))

    def takes(j):
        return ((group == 1) | (group == 3), group >= 2, group == 3)[j]

    def total_arrived(c, j):
        arrived(urecv.at[c, j], B + later * c + j)

    def peer(j):
        chip, flip = PEERS[j - 1]
        core = lax.rem(head, 2)
        there = lax.rem(head // 2 + chip, n_head // 2)
        return 2 * there + (1 - core if flip else core)

    def put(src, dst, which, device, lands=None):
        pltpu.make_async_remote_copy(
            src_ref=src,
            dst_ref=dst,
            send_sem=send_sem.at[which],
            recv_sem=recv_sem.at[which if lands is None else lands],
            device_id=device,
            device_id_type=MESH,
        ).start()

    def arrived(ref, which):
        pltpu.make_async_copy(ref, ref, recv_sem.at[which]).wait()

    def sent(ref, which):
        pltpu.make_async_copy(ref, ref, send_sem.at[which]).wait()

    def local(src, dst, which):
        pltpu.make_async_copy(src, dst, recv_sem.at[which]).start()

    local(ig_ref, gates.at[0], GATE)
    local(fg_ref, gates.at[1], GATE)

    barrier = pltpu.get_barrier_semaphore()

    def greet(j, there):
        pl.semaphore_signal(barrier, inc=1, device_id=(there, head), device_id_type=MESH)

    each_later(greet)
    for j in range(1, MEMBERS):
        pl.semaphore_signal(barrier, inc=1, device_id=(member(j), head), device_id_type=MESH)
    for j in range(1, n_head):
        pl.semaphore_signal(barrier, inc=1, device_id=(seq, peer(j)), device_id_type=MESH)

    def key_cols(h):
        return pl.ds(pl.multiple_of(h * key_dim, key_dim), key_dim)

    def value_cols(h, c):
        return pl.ds(pl.multiple_of(h * value_dim + c * width, width), width)

    my_rows = pl.ds(head_row, tok)
    local(k_ref.at[:, key_cols(head)], kbuf.at[my_rows], K)
    for c in range(CHUNKS):
        local(v_ref.at[:, value_cols(head, c)], vbuf.at[c, my_rows], V + c)
    local(q_ref.at[:, key_cols(head)], qbuf.at[my_rows], Q)

    for j in range(later):

        @pl.when(j >= group)
        def _():
            hdr_total_all[j] = jnp.zeros(hdr_total.shape, jnp.float32)

        @pl.when(jnp.logical_not(takes(j)))
        def _():
            for c in range(CHUNKS):
                urecv[c, j] = jnp.zeros(urecv.shape[2:], urecv.dtype)

    pl.semaphore_wait(barrier, n_head - 1 + MEMBERS - 1 + group)

    def answer(j, there):
        pl.semaphore_signal(relay_sem, inc=1, device_id=(there, head), device_id_type=MESH)

    each_earlier(answer)

    for j in range(1, n_head):
        h = peer(j)
        put(k_ref.at[:, key_cols(h)], kbuf.at[my_rows], K, (seq, h))
    for c in range(CHUNKS):
        for j in range(1, n_head):
            h = peer(j)
            put(v_ref.at[:, value_cols(h, c)], vbuf.at[c, my_rows], V + c, (seq, h))
    for j in range(1, n_head):
        h = peer(j)
        put(q_ref.at[:, key_cols(h)], qbuf.at[my_rows], Q, (seq, h))

    arrived(gates, GATE)
    gate = gates[0]
    forget = gates[1]
    log_keep = jnp.minimum(forget, 0.0) - jnp.log1p(jnp.exp(-jnp.abs(forget)))
    lane = lax.broadcasted_iota(jnp.int32, (8, rows), 1)
    within_row = jnp.broadcast_to(log_keep, (8, rows))
    step = 1
    while step < rows:
        within_row = within_row + jnp.where(lane >= step, pltpu.roll(within_row, step, 1), 0.0)
        step *= 2
    within_row = within_row[0:1, :]
    decay = within_row[:, rows - 1 : rows]
    gate_less = gate - within_row

    def gate_tile(i, peak):
        at = pl.ds(pl.multiple_of(i * TILE, TILE), TILE)
        t = lax.broadcasted_iota(jnp.int32, (TILE, rows), 0) + i * TILE
        s = lax.broadcasted_iota(jnp.int32, (TILE, rows), 1)
        col = jnp.sum(jnp.where(s <= t, log_keep, 0.0), axis=1, keepdims=True)
        own_gate = jnp.sum(jnp.where(s == t, gate, 0.0), axis=1, keepdims=True)
        since = decay - col + own_gate
        within_col[at, :] = col
        weight_col[at, :] = since
        local_max[at, :] = col + jnp.max(
            jnp.where(s <= t, gate_less, NEG_FILL), axis=1, keepdims=True
        )
        return jnp.maximum(peak, jnp.max(since, axis=0, keepdims=True))

    peak_own = lax.fori_loop(
        0, rows // TILE, gate_tile, jnp.full((1, 1), -jnp.inf, jnp.float32)
    )
    hdr[...] = jnp.zeros_like(hdr)
    hdr[0:1, :] = jnp.broadcast_to(decay, (1, 128))
    hdr[1:2, :] = jnp.broadcast_to(peak_own, (1, 128))
    hdr_total[...] = jnp.zeros_like(hdr_total)
    nrm[...] = jnp.zeros_like(nrm)
    hdr_all[me] = hdr[...]
    for j in range(1, MEMBERS):
        put(hdr, hdr_all.at[me], HDR, (member(j), head))

    arrived(kbuf, K)

    def key_tile(i, normal):
        at = pl.ds(pl.multiple_of(i * TILE, TILE), TILE)
        weight = jnp.exp(weight_col[at, :] - peak_own)
        weighted = weight * kbuf[at, :].astype(jnp.float32)
        wkt[:, at] = weighted.T.astype(jnp.bfloat16)
        return normal + jnp.sum(weighted, axis=0, keepdims=True)

    normal_own = lax.fori_loop(
        0, rows // TILE, key_tile, jnp.zeros((1, key_dim), jnp.float32)
    )
    for i in range(key_dim // 128):
        nrm[2 + i : 3 + i, :] = normal_own[:, i * 128 : (i + 1) * 128]
    nrm_all[me] = nrm[...]
    for j in range(1, MEMBERS):
        put(nrm, nrm_all.at[me], NRM, (member(j), head))

    norm_rows = slice(2, 2 + key_dim // 128)
    no_peak = jnp.full((1, 128), NEG_FILL, jnp.float32)
    no_norm = jnp.zeros((key_dim // 128, 128), jnp.float32)

    arrived(hdr_all.at[pl.ds(0, MEMBERS - 1)], HDR)
    peak, total = no_peak, jnp.zeros((1, 128), jnp.float32)
    for g in range(MEMBERS):
        d, p = hdr_all[g, 0:1, :], hdr_all[g, 1:2, :]
        new = jnp.maximum(d + peak, p)
        coef_local[g, 0:1, :] = jnp.exp(d + peak - new)
        coef_local[g, 1:2, :] = jnp.exp(p - new)
        peak, total = new, total + d
    hdr_total[0:1, :] = total
    hdr_total[1:2, :] = peak

    for c in range(CHUNKS):
        arrived(vbuf.at[c], V + c)
        own = jnp.dot(wkt[...], vbuf[c], preferred_element_type=jnp.float32)
        mown[c] = own.astype(jnp.bfloat16).reshape(MEMBERS, part, width)
        for j in range(1, MEMBERS):
            g = lax.rem(me + j, MEMBERS)
            owned = lax.rem(g + turned, MEMBERS)
            put(mown.at[c, owned], mrecv.at[c, me], A + c, (base + g, head))
        mrecv[c, me] = mown[c, mine]

    arrived(nrm_all.at[pl.ds(0, MEMBERS - 1)], NRM)
    norm = no_norm
    for g in range(MEMBERS):
        norm = coef_local[g, 0:1, :] * norm + coef_local[g, 1:2, :] * nrm_all[g, norm_rows, :]
    hdr_total[norm_rows, :] = norm
    hdr_total_all[group] = hdr_total[...]

    @pl.when(group < later)
    def _():
        pl.semaphore_wait(relay_sem, later - group)

    def send_header(j, there):
        put(hdr_total, hdr_total_all.at[group], HDRT + j - 1, (there, head), HDRT + group)

    each_later(send_header)

    scale = key_dim ** (-0.5)

    def score_tile(i, carry):
        at = pl.ds(pl.multiple_of(i * TILE, TILE), TILE)
        scores[at, :] = lax.dot_general(
            qbuf[at, :], kbuf[...], (((1,), (1,)), ((), ())), preferred_element_type=jnp.float32
        )
        return carry

    def wide(row):
        return jnp.concatenate([row] * (width // 128), axis=1)

    def full_headers():
        each_earlier(lambda j, there: arrived(hdr_total_all.at[j], HDRT + j))
        peak, norm = no_peak, no_norm
        for j in range(n_group - 1):
            d, p = hdr_total_all[j, 0:1, :], hdr_total_all[j, 1:2, :]
            new = jnp.maximum(d + peak, p)
            used = j < group
            older, newer = jnp.exp(d + peak - new), jnp.exp(p - new)
            coef_total[j, 0:1, :] = older
            coef_total[j, 1:2, :] = newer
            norm = jnp.where(used, older * norm + newer * hdr_total_all[j, norm_rows, :], norm)
            peak = jnp.where(used, new, peak)
        for g in range(MEMBERS):
            entry[g, 1:2, :] = peak
            entry[g, norm_rows, :] = norm
            d, p = hdr_all[g, 0:1, :], hdr_all[g, 1:2, :]
            new = jnp.maximum(d + peak, p)
            older, newer = jnp.exp(d + peak - new), jnp.exp(p - new)
            coef_full[g, 0:1, :] = older
            coef_full[g, 1:2, :] = newer
            norm = older * norm + newer * nrm_all[g, norm_rows, :]
            peak = new

    def send_totals(c):
        arrived(mrecv.at[c, pl.ds(0, MEMBERS - 1)], A + c)

        @pl.when(group < later)
        def _():
            state = jnp.zeros((part, width), jnp.float32)
            for g in range(MEMBERS):
                state = (
                    wide(coef_local[g, 0:1, :]) * state
                    + wide(coef_local[g, 1:2, :]) * mrecv[c, g].astype(jnp.float32)
                )
            usend[c] = state.astype(jnp.bfloat16)

            def send_total(src, j):
                at = B + later * c
                put(src, urecv.at[c, group], at + j - 1, (owner_later(j), head), at + group)

            pl.when(group == 0)(functools.partial(send_total, usend.at[c], 3))
            pl.when(group == 1)(functools.partial(send_total, usend.at[c], 2))
            pl.when(group != 1)(functools.partial(send_total, usend.at[c], 1))

            @pl.when(group == 1)
            def _():
                total_arrived(c, 0)
                umerged[c] = (
                    wide(coef_total[1, 0:1, :]) * urecv[c, 0].astype(jnp.float32)
                    + wide(coef_total[1, 1:2, :]) * state
                ).astype(jnp.bfloat16)
                send_total(umerged.at[c], 1)

    def send_entering(c):
        pl.when(group == 3)(functools.partial(total_arrived, c, 0))
        for j in range(1, later):
            pl.when(takes(j))(functools.partial(total_arrived, c, j))
        came = [urecv[c, j].astype(jnp.float32) for j in range(later)]
        every = came[0]
        for j in range(1, later):
            every = wide(coef_total[j, 0:1, :]) * every + wide(coef_total[j, 1:2, :]) * came[j]
        state = jnp.where(group == 3, every, jnp.where(group == 2, came[1], came[0]))
        for g in range(MEMBERS):
            isend[c, g] = state.astype(jnp.bfloat16)
            state = (
                wide(coef_full[g, 0:1, :]) * state
                + wide(coef_full[g, 1:2, :]) * mrecv[c, g].astype(jnp.float32)
            )
        my_part = pl.ds(pl.multiple_of(mine * part, part), part)
        for j in range(1, MEMBERS):
            g = lax.rem(me + j, MEMBERS)
            put(isend.at[c, g], irecv.at[c, my_part], C + c, (base + g, head))
        irecv[c, my_part] = isend[c, me]

    pl.when(group < 2)(full_headers)
    for c in range(CHUNKS):
        send_totals(c)
        if c >= LAG:
            pl.when(group < 2)(functools.partial(send_entering, c - LAG))
    pl.when(group >= 2)(full_headers)
    for c in range(CHUNKS):
        if c >= CHUNKS - LAG:
            send_entering(c)
        else:
            pl.when(group >= 2)(functools.partial(send_entering, c))
    arrived(qbuf, Q)
    lax.fori_loop(0, rows // TILE, score_tile, 0)

    my_entry = entry[me]
    peak_in = my_entry[1:2, 0:1]
    normal_in = jnp.concatenate(
        [my_entry[2 + i : 3 + i, :] for i in range(key_dim // 128)], axis=1
    )

    def mixing_tile(i, carry):
        at = pl.ds(pl.multiple_of(i * TILE, TILE), TILE)
        t = lax.broadcasted_iota(jnp.int32, (TILE, rows), 0) + i * TILE
        s = lax.broadcasted_iota(jnp.int32, (TILE, rows), 1)
        col = within_col[at, :]
        entry_log = col + peak_in
        peak_row = jnp.maximum(entry_log, local_max[at, :])
        logs = jnp.where(s <= t, (col - peak_row) + gate_less, NEG_FILL)
        mix = jnp.exp(logs) * (scores[at, :] * scale)
        mixing[at, :] = mix.astype(jnp.bfloat16)
        rate = jnp.exp(entry_log - peak_row)
        from_normal = jnp.sum(
            qbuf[at, :].astype(jnp.float32) * normal_in, axis=1, keepdims=True
        )
        below = jnp.sum(mix, axis=1, keepdims=True) + rate * (from_normal * scale)
        inverse = 1.0 / jnp.maximum(jnp.abs(below), 1.0)
        entry_rate[at, 0:1] = rate * inverse * scale
        entry_rate[at, 1:2] = inverse
        return carry

    lax.fori_loop(0, rows // TILE, mixing_tile, 0)

    def local_tile(i, carry):
        at = pl.ds(pl.multiple_of(i * TILE, TILE), TILE)
        for c in range(CHUNKS):
            local_out[c, at, :] = entry_rate[at, 1:2] * jnp.dot(
                mixing[at, :], vbuf[c], preferred_element_type=jnp.float32
            )
        return carry

    lax.fori_loop(0, rows // TILE, local_tile, 0)

    def send_hidden(c, h):
        put(
            hid.at[c, pl.ds(pl.multiple_of(h * tok, tok), tok)],
            ret_ref.at[:, value_cols(head, c)],
            R + c,
            (seq, h),
        )

    for c in range(CHUNKS):
        arrived(irecv.at[c, pl.ds(0, key_dim - part)], C + c)

        for i in range(n_head // 2 - 1, -1, -1):
            chip = lax.rem(head // 2 + (i + 1) % (n_head // 2), n_head // 2)
            at = pl.ds(pl.multiple_of(chip * 2 * tok, 2 * tok), 2 * tok)
            from_memory = jnp.dot(
                qbuf[at, :], irecv[c], preferred_element_type=jnp.float32
            )
            hid[c, at, :] = (
                local_out[c, at, :] + entry_rate[at, 0:1] * from_memory
            ).astype(jnp.bfloat16)
            for core in range(2):
                h = 2 * chip + core
                pl.when(h != head)(functools.partial(send_hidden, c, h))
        local(hid.at[c, my_rows], ret_ref.at[:, value_cols(head, c)], R + c)

    for c in range(CHUNKS):
        arrived(hid.at[c], R + c)

    peers_rows = pl.ds(0, rows - tok)
    sent(kbuf.at[peers_rows], K)
    sent(qbuf.at[peers_rows], Q)
    sent(hdr_all.at[pl.ds(0, MEMBERS - 1)], HDR)
    sent(nrm_all.at[pl.ds(0, MEMBERS - 1)], NRM)
    each_later(lambda j, there: sent(hdr_total, HDRT + j - 1))
    for c in range(CHUNKS):
        sent(vbuf.at[c, peers_rows], V + c)
        sent(mrecv.at[c, pl.ds(0, MEMBERS - 1)], A + c)
        pl.when(group < later)(lambda: sent(usend.at[c], B + later * c))
        pl.when(group == 1)(lambda: sent(usend.at[c], B + later * c + 1))
        pl.when(group == 0)(lambda: sent(usend.at[c], B + later * c + 2))
        sent(irecv.at[c, pl.ds(0, key_dim - part)], C + c)
        sent(hid.at[c, peers_rows], R + c)


def per_device(n_seq, n_head, queries, keys, values, in_gate, forget_gate, out_gate):
    tok = queries.shape[0]
    rows = tok * n_head
    key_dim = queries.shape[1] // n_head
    value_dim = values.shape[1] // n_head
    width = value_dim // CHUNKS
    part = key_dim // MEMBERS
    n_group = n_seq // MEMBERS
    bf16, f32 = jnp.bfloat16, jnp.float32
    n_sem = 5 + 4 * CHUNKS + (n_group - 1) * (1 + CHUNKS)
    scratch = [
        pltpu.VMEM((2, 1, rows), f32),
        pltpu.VMEM((rows, key_dim), bf16),
        pltpu.VMEM((rows, key_dim), bf16),
        pltpu.VMEM((CHUNKS, rows, width), bf16),
        pltpu.VMEM((key_dim, rows), bf16),
        pltpu.VMEM((rows, 1), f32),
        pltpu.VMEM((rows, 1), f32),
        pltpu.VMEM((rows, 1), f32),
        pltpu.VMEM((rows, rows), f32),
        pltpu.VMEM((rows, rows), bf16),
        pltpu.VMEM((rows, 2), f32),
        pltpu.VMEM((CHUNKS, rows, width), f32),
        pltpu.VMEM((8, 128), f32),
        pltpu.VMEM((MEMBERS, 8, 128), f32),
        pltpu.VMEM((8, 128), f32),
        pltpu.VMEM((MEMBERS, 8, 128), f32),
        pltpu.VMEM((8, 128), f32),
        pltpu.VMEM((n_group, 8, 128), f32),
        pltpu.VMEM((MEMBERS, 8, 128), f32),
        pltpu.VMEM((MEMBERS, 8, 128), f32),
        pltpu.VMEM((MEMBERS, 8, 128), f32),
        pltpu.VMEM((n_group, 8, 128), f32),
        pltpu.VMEM((CHUNKS, MEMBERS, part, width), bf16),
        pltpu.VMEM((CHUNKS, MEMBERS, part, width), bf16),
        pltpu.VMEM((CHUNKS, part, width), bf16),
        pltpu.VMEM((CHUNKS, part, width), bf16),
        pltpu.VMEM((CHUNKS, n_group, part, width), bf16),
        pltpu.VMEM((CHUNKS, MEMBERS, part, width), bf16),
        pltpu.VMEM((CHUNKS, key_dim, width), bf16),
        pltpu.VMEM((CHUNKS, rows, width), bf16),
        pltpu.SemaphoreType.DMA((n_sem,)),
        pltpu.SemaphoreType.DMA((n_sem,)),
        pltpu.SemaphoreType.REGULAR,
    ]
    anywhere = pl.BlockSpec(memory_space=pl.ANY)
    hbm = pl.BlockSpec(memory_space=pltpu.HBM)
    returned = pl.pallas_call(
        functools.partial(kernel, (n_seq, n_head)),
        out_shape=pltpu.VMEM((tok, n_head * value_dim), bf16),
        in_specs=[hbm] * 5,
        out_specs=pl.BlockSpec(memory_space=pltpu.VMEM),
        scratch_shapes=scratch,
        compiler_params=pltpu.CompilerParams(
            collective_id=0, has_side_effects=True, vmem_limit_bytes=60 * 2**20
        ),
    )(queries, keys, values, in_gate, forget_gate)
    gated = jax.nn.sigmoid(out_gate.astype(f32)) * returned.astype(f32)
    return gated.astype(bf16)


def solution(mesh):
    return jax.shard_map(
        functools.partial(per_device, mesh.shape["seq"], mesh.shape["head"]),
        mesh=mesh,
        in_specs=(
            P(("seq", "head"), None),
            P(("seq", "head"), None),
            P(("seq", "head"), None),
            P("head", "seq"),
            P("head", "seq"),
            P(("seq", "head"), None),
        ),
        out_specs=P(("seq", "head"), None),
        check_vma=False,
    )
```

```python
import functools

import jax
import jax.numpy as jnp
from jax import lax
from jax.experimental import pallas as pl
from jax.experimental.pallas import tpu as pltpu
from jax.sharding import PartitionSpec as P

MESH = pl.DeviceIdType.MESH
NEG_FILL = -1e30
MEMBERS = 16
CHUNKS = 4
TILE = 128
LAG = 2
PEERS = ((2, 0), (1, 0), (3, 0), (2, 1), (1, 1), (3, 1), (0, 1))


def kernel(
    sizes,
    q_ref,
    k_ref,
    v_ref,
    ig_ref,
    fg_ref,
    ret_ref,
    gates,
    qbuf,
    kbuf,
    vbuf,
    wkt,
    within_col,
    weight_col,
    local_max,
    scores,
    mixing,
    entry_rate,
    local_out,
    hdr,
    hdr_all,
    nrm,
    nrm_all,
    hdr_total,
    hdr_total_all,
    coef_local,
    coef_full,
    entry,
    coef_total,
    mown,
    mrecv,
    usend,
    umerged,
    urecv,
    isend,
    irecv,
    hid,
    send_sem,
    recv_sem,
    relay_sem,
):
    n_seq, n_head = sizes
    n_group = n_seq // MEMBERS
    tok = q_ref.shape[0]
    rows, key_dim = kbuf.shape
    width = vbuf.shape[2]
    value_dim = width * CHUNKS
    part = key_dim // MEMBERS
    seq = lax.axis_index("seq")
    head = lax.axis_index("head")
    me = lax.rem(seq, MEMBERS)
    group = seq // MEMBERS
    base = group * MEMBERS
    head_row = pl.multiple_of(head * tok, tok)

    later = n_group - 1
    K, Q, HDR, NRM, GATE = range(5)
    V, A, C, R = (5 + CHUNKS * i for i in range(4))
    HDRT = 5 + 4 * CHUNKS
    B = HDRT + later

    turned = jnp.where(group == later, MEMBERS // 2, 0)
    mine = lax.rem(me + turned, MEMBERS)

    def member(j):
        return base + lax.rem(me + j, MEMBERS)

    def owner_later(j):
        turn = jnp.where(group + j == later, MEMBERS // 2, 0)
        return (group + j) * MEMBERS + lax.rem(me + turn, MEMBERS)

    def each_later(act):
        for j in (2, 3, 1):
            pl.when(group + j < n_group)(functools.partial(act, j, owner_later(j)))

    def each_earlier(act):
        for j in range(later):
            pl.when(j < group)(functools.partial(act, j, j * MEMBERS + mine))

    def takes(j):
        return ((group == 1) | (group == 3), group >= 2, group == 3)[j]

    def total_arrived(c, j):
        arrived(urecv.at[c, j], B + later * c + j)

    def peer(j):
        chip, flip = PEERS[j - 1]
        core = lax.rem(head, 2)
        there = lax.rem(head // 2 + chip, n_head // 2)
        return 2 * there + (1 - core if flip else core)

    def put(src, dst, which, device, lands=None):
        pltpu.make_async_remote_copy(
            src_ref=src,
            dst_ref=dst,
            send_sem=send_sem.at[which],
            recv_sem=recv_sem.at[which if lands is None else lands],
            device_id=device,
            device_id_type=MESH,
        ).start()

    def arrived(ref, which):
        pltpu.make_async_copy(ref, ref, recv_sem.at[which]).wait()

    def sent(ref, which):
        pltpu.make_async_copy(ref, ref, send_sem.at[which]).wait()

    def local(src, dst, which):
        pltpu.make_async_copy(src, dst, recv_sem.at[which]).start()

    local(ig_ref, gates.at[0], GATE)
    local(fg_ref, gates.at[1], GATE)

    barrier = pltpu.get_barrier_semaphore()

    def greet(j, there):
        pl.semaphore_signal(barrier, inc=1, device_id=(there, head), device_id_type=MESH)

    each_later(greet)
    for j in range(1, MEMBERS):
        pl.semaphore_signal(barrier, inc=1, device_id=(member(j), head), device_id_type=MESH)
    for j in range(1, n_head):
        pl.semaphore_signal(barrier, inc=1, device_id=(seq, peer(j)), device_id_type=MESH)

    def key_cols(h):
        return pl.ds(pl.multiple_of(h * key_dim, key_dim), key_dim)

    def value_cols(h, c):
        return pl.ds(pl.multiple_of(h * value_dim + c * width, width), width)

    my_rows = pl.ds(head_row, tok)
    local(k_ref.at[:, key_cols(head)], kbuf.at[my_rows], K)
    for c in range(CHUNKS):
        local(v_ref.at[:, value_cols(head, c)], vbuf.at[c, my_rows], V + c)
    local(q_ref.at[:, key_cols(head)], qbuf.at[my_rows], Q)

    for j in range(later):

        @pl.when(j >= group)
        def _():
            hdr_total_all[j] = jnp.zeros(hdr_total.shape, jnp.float32)

        @pl.when(jnp.logical_not(takes(j)))
        def _():
            for c in range(CHUNKS):
                urecv[c, j] = jnp.zeros(urecv.shape[2:], urecv.dtype)

    pl.semaphore_wait(barrier, n_head - 1 + MEMBERS - 1 + group)

    def answer(j, there):
        pl.semaphore_signal(relay_sem, inc=1, device_id=(there, head), device_id_type=MESH)

    each_earlier(answer)

    for j in range(1, n_head):
        h = peer(j)
        put(k_ref.at[:, key_cols(h)], kbuf.at[my_rows], K, (seq, h))
    for c in range(CHUNKS):
        for j in range(1, n_head):
            h = peer(j)
            put(v_ref.at[:, value_cols(h, c)], vbuf.at[c, my_rows], V + c, (seq, h))
    arrived(gates, GATE)
    gate = gates[0]
    forget = gates[1]
    log_keep = jnp.minimum(forget, 0.0) - jnp.log1p(jnp.exp(-jnp.abs(forget)))
    lane = lax.broadcasted_iota(jnp.int32, (8, rows), 1)
    within_row = jnp.broadcast_to(log_keep, (8, rows))
    step = 1
    while step < rows:
        within_row = within_row + jnp.where(lane >= step, pltpu.roll(within_row, step, 1), 0.0)
        step *= 2
    within_row = within_row[0:1, :]
    decay = within_row[:, rows - 1 : rows]
    gate_less = gate - within_row

    def gate_tile(i, peak):
        at = pl.ds(pl.multiple_of(i * TILE, TILE), TILE)
        t = lax.broadcasted_iota(jnp.int32, (TILE, rows), 0) + i * TILE
        s = lax.broadcasted_iota(jnp.int32, (TILE, rows), 1)
        col = jnp.sum(jnp.where(s <= t, log_keep, 0.0), axis=1, keepdims=True)
        own_gate = jnp.sum(jnp.where(s == t, gate, 0.0), axis=1, keepdims=True)
        since = decay - col + own_gate
        within_col[at, :] = col
        weight_col[at, :] = since
        local_max[at, :] = col + jnp.max(
            jnp.where(s <= t, gate_less, NEG_FILL), axis=1, keepdims=True
        )
        return jnp.maximum(peak, jnp.max(since, axis=0, keepdims=True))

    peak_own = lax.fori_loop(
        0, rows // TILE, gate_tile, jnp.full((1, 1), -jnp.inf, jnp.float32)
    )
    hdr[...] = jnp.zeros_like(hdr)
    hdr[0:1, :] = jnp.broadcast_to(decay, (1, 128))
    hdr[1:2, :] = jnp.broadcast_to(peak_own, (1, 128))
    hdr_total[...] = jnp.zeros_like(hdr_total)
    nrm[...] = jnp.zeros_like(nrm)
    hdr_all[me] = hdr[...]
    for j in range(1, MEMBERS):
        put(hdr, hdr_all.at[me], HDR, (member(j), head))

    arrived(kbuf, K)

    def key_tile(i, normal):
        at = pl.ds(pl.multiple_of(i * TILE, TILE), TILE)
        weight = jnp.exp(weight_col[at, :] - peak_own)
        weighted = weight * kbuf[at, :].astype(jnp.float32)
        wkt[:, at] = weighted.T.astype(jnp.bfloat16)
        return normal + jnp.sum(weighted, axis=0, keepdims=True)

    normal_own = lax.fori_loop(
        0, rows // TILE, key_tile, jnp.zeros((1, key_dim), jnp.float32)
    )
    for i in range(key_dim // 128):
        nrm[2 + i : 3 + i, :] = normal_own[:, i * 128 : (i + 1) * 128]
    nrm_all[me] = nrm[...]
    for j in range(1, MEMBERS):
        put(nrm, nrm_all.at[me], NRM, (member(j), head))

    norm_rows = slice(2, 2 + key_dim // 128)
    no_peak = jnp.full((1, 128), NEG_FILL, jnp.float32)
    no_norm = jnp.zeros((key_dim // 128, 128), jnp.float32)

    arrived(hdr_all.at[pl.ds(0, MEMBERS - 1)], HDR)
    peak, total = no_peak, jnp.zeros((1, 128), jnp.float32)
    for g in range(MEMBERS):
        d, p = hdr_all[g, 0:1, :], hdr_all[g, 1:2, :]
        new = jnp.maximum(d + peak, p)
        coef_local[g, 0:1, :] = jnp.exp(d + peak - new)
        coef_local[g, 1:2, :] = jnp.exp(p - new)
        peak, total = new, total + d
    hdr_total[0:1, :] = total
    hdr_total[1:2, :] = peak

    for c in range(CHUNKS):
        arrived(vbuf.at[c], V + c)
        own = jnp.dot(wkt[...], vbuf[c], preferred_element_type=jnp.float32)
        mown[c] = own.astype(jnp.bfloat16).reshape(MEMBERS, part, width)
        for j in range(1, MEMBERS):
            g = lax.rem(me + j, MEMBERS)
            owned = lax.rem(g + turned, MEMBERS)
            put(mown.at[c, owned], mrecv.at[c, me], A + c, (base + g, head))
        mrecv[c, me] = mown[c, mine]
        if c == CHUNKS - 2:
            for j in range(1, n_head):
                h = peer(j)
                put(q_ref.at[:, key_cols(h)], qbuf.at[my_rows], Q, (seq, h))

    arrived(nrm_all.at[pl.ds(0, MEMBERS - 1)], NRM)
    norm = no_norm
    for g in range(MEMBERS):
        norm = coef_local[g, 0:1, :] * norm + coef_local[g, 1:2, :] * nrm_all[g, norm_rows, :]
    hdr_total[norm_rows, :] = norm
    hdr_total_all[group] = hdr_total[...]

    @pl.when(group < later)
    def _():
        pl.semaphore_wait(relay_sem, later - group)

    def send_header(j, there):
        put(hdr_total, hdr_total_all.at[group], HDRT + j - 1, (there, head), HDRT + group)

    each_later(send_header)

    scale = key_dim ** (-0.5)

    def score_tile(i, carry):
        at = pl.ds(pl.multiple_of(i * TILE, TILE), TILE)
        scores[at, :] = lax.dot_general(
            qbuf[at, :], kbuf[...], (((1,), (1,)), ((), ())), preferred_element_type=jnp.float32
        )
        return carry

    def wide(row):
        return jnp.concatenate([row] * (width // 128), axis=1)

    def full_headers():
        each_earlier(lambda j, there: arrived(hdr_total_all.at[j], HDRT + j))
        peak, norm = no_peak, no_norm
        for j in range(n_group - 1):
            d, p = hdr_total_all[j, 0:1, :], hdr_total_all[j, 1:2, :]
            new = jnp.maximum(d + peak, p)
            used = j < group
            older, newer = jnp.exp(d + peak - new), jnp.exp(p - new)
            coef_total[j, 0:1, :] = older
            coef_total[j, 1:2, :] = newer
            norm = jnp.where(used, older * norm + newer * hdr_total_all[j, norm_rows, :], norm)
            peak = jnp.where(used, new, peak)
        for g in range(MEMBERS):
            entry[g, 1:2, :] = peak
            entry[g, norm_rows, :] = norm
            d, p = hdr_all[g, 0:1, :], hdr_all[g, 1:2, :]
            new = jnp.maximum(d + peak, p)
            older, newer = jnp.exp(d + peak - new), jnp.exp(p - new)
            coef_full[g, 0:1, :] = older
            coef_full[g, 1:2, :] = newer
            norm = older * norm + newer * nrm_all[g, norm_rows, :]
            peak = new

    def send_totals(c):
        arrived(mrecv.at[c, pl.ds(0, MEMBERS - 1)], A + c)

        @pl.when(group < later)
        def _():
            state = jnp.zeros((part, width), jnp.float32)
            for g in range(MEMBERS):
                state = (
                    wide(coef_local[g, 0:1, :]) * state
                    + wide(coef_local[g, 1:2, :]) * mrecv[c, g].astype(jnp.float32)
                )
            usend[c] = state.astype(jnp.bfloat16)

            def send_total(src, j):
                at = B + later * c
                put(src, urecv.at[c, group], at + j - 1, (owner_later(j), head), at + group)

            pl.when(group == 0)(functools.partial(send_total, usend.at[c], 3))
            pl.when(group == 1)(functools.partial(send_total, usend.at[c], 2))
            pl.when(group != 1)(functools.partial(send_total, usend.at[c], 1))

            @pl.when(group == 1)
            def _():
                total_arrived(c, 0)
                umerged[c] = (
                    wide(coef_total[1, 0:1, :]) * urecv[c, 0].astype(jnp.float32)
                    + wide(coef_total[1, 1:2, :]) * state
                ).astype(jnp.bfloat16)
                send_total(umerged.at[c], 1)

    def send_entering(c):
        pl.when(group == 3)(functools.partial(total_arrived, c, 0))
        for j in range(1, later):
            pl.when(takes(j))(functools.partial(total_arrived, c, j))
        came = [urecv[c, j].astype(jnp.float32) for j in range(later)]
        every = came[0]
        for j in range(1, later):
            every = wide(coef_total[j, 0:1, :]) * every + wide(coef_total[j, 1:2, :]) * came[j]
        state = jnp.where(group == 3, every, jnp.where(group == 2, came[1], came[0]))
        for g in range(MEMBERS):
            isend[c, g] = state.astype(jnp.bfloat16)
            state = (
                wide(coef_full[g, 0:1, :]) * state
                + wide(coef_full[g, 1:2, :]) * mrecv[c, g].astype(jnp.float32)
            )
        my_part = pl.ds(pl.multiple_of(mine * part, part), part)
        for j in range(1, MEMBERS):
            g = lax.rem(me + j, MEMBERS)
            put(isend.at[c, g], irecv.at[c, my_part], C + c, (base + g, head))
        irecv[c, my_part] = isend[c, me]

    pl.when(group < 2)(full_headers)
    for c in range(CHUNKS):
        send_totals(c)
        if c >= LAG:
            pl.when(group < 2)(functools.partial(send_entering, c - LAG))
    pl.when(group >= 2)(full_headers)
    arrived(qbuf, Q)
    pl.when(group == 3)(lambda: lax.fori_loop(0, rows // TILE, score_tile, None))
    for c in range(CHUNKS):
        if c >= CHUNKS - LAG:
            send_entering(c)
        else:
            pl.when(group >= 2)(functools.partial(send_entering, c))
    pl.when(group < 3)(lambda: lax.fori_loop(0, rows // TILE, score_tile, None))

    my_entry = entry[me]
    peak_in = my_entry[1:2, 0:1]
    normal_in = jnp.concatenate(
        [my_entry[2 + i : 3 + i, :] for i in range(key_dim // 128)], axis=1
    )

    def mixing_tile(i, carry):
        at = pl.ds(pl.multiple_of(i * TILE, TILE), TILE)
        t = lax.broadcasted_iota(jnp.int32, (TILE, rows), 0) + i * TILE
        s = lax.broadcasted_iota(jnp.int32, (TILE, rows), 1)
        col = within_col[at, :]
        entry_log = col + peak_in
        peak_row = jnp.maximum(entry_log, local_max[at, :])
        logs = jnp.where(s <= t, (col - peak_row) + gate_less, NEG_FILL)
        mix = jnp.exp(logs) * (scores[at, :] * scale)
        mixing[at, :] = mix.astype(jnp.bfloat16)
        rate = jnp.exp(entry_log - peak_row)
        from_normal = jnp.sum(
            qbuf[at, :].astype(jnp.float32) * normal_in, axis=1, keepdims=True
        )
        below = jnp.sum(mix, axis=1, keepdims=True) + rate * (from_normal * scale)
        inverse = 1.0 / jnp.maximum(jnp.abs(below), 1.0)
        entry_rate[at, 0:1] = rate * inverse * scale
        entry_rate[at, 1:2] = inverse
        return carry

    lax.fori_loop(0, rows // TILE, mixing_tile, 0)

    def local_tile(i, carry):
        at = pl.ds(pl.multiple_of(i * TILE, TILE), TILE)
        for c in range(CHUNKS):
            local_out[c, at, :] = entry_rate[at, 1:2] * jnp.dot(
                mixing[at, :], vbuf[c], preferred_element_type=jnp.float32
            )
        return carry

    lax.fori_loop(0, rows // TILE, local_tile, 0)

    def send_hidden(c, h):
        put(
            hid.at[c, pl.ds(pl.multiple_of(h * tok, tok), tok)],
            ret_ref.at[:, value_cols(head, c)],
            R + c,
            (seq, h),
        )

    for c in range(CHUNKS):
        arrived(irecv.at[c, pl.ds(0, key_dim - part)], C + c)

        for i in range(n_head // 2 - 1, -1, -1):
            chip = lax.rem(head // 2 + (i + 1) % (n_head // 2), n_head // 2)
            at = pl.ds(pl.multiple_of(chip * 2 * tok, 2 * tok), 2 * tok)
            from_memory = jnp.dot(
                qbuf[at, :], irecv[c], preferred_element_type=jnp.float32
            )
            hid[c, at, :] = (
                local_out[c, at, :] + entry_rate[at, 0:1] * from_memory
            ).astype(jnp.bfloat16)
            for core in range(2):
                h = 2 * chip + core
                pl.when(h != head)(functools.partial(send_hidden, c, h))
        local(hid.at[c, my_rows], ret_ref.at[:, value_cols(head, c)], R + c)

    for c in range(CHUNKS):
        arrived(hid.at[c], R + c)

    peers_rows = pl.ds(0, rows - tok)
    sent(kbuf.at[peers_rows], K)
    sent(qbuf.at[peers_rows], Q)
    sent(hdr_all.at[pl.ds(0, MEMBERS - 1)], HDR)
    sent(nrm_all.at[pl.ds(0, MEMBERS - 1)], NRM)
    each_later(lambda j, there: sent(hdr_total, HDRT + j - 1))
    for c in range(CHUNKS):
        sent(vbuf.at[c, peers_rows], V + c)
        sent(mrecv.at[c, pl.ds(0, MEMBERS - 1)], A + c)
        pl.when(group < later)(lambda: sent(usend.at[c], B + later * c))
        pl.when(group == 1)(lambda: sent(usend.at[c], B + later * c + 1))
        pl.when(group == 0)(lambda: sent(usend.at[c], B + later * c + 2))
        sent(irecv.at[c, pl.ds(0, key_dim - part)], C + c)
        sent(hid.at[c, peers_rows], R + c)


def per_device(n_seq, n_head, queries, keys, values, in_gate, forget_gate, out_gate):
    tok = queries.shape[0]
    rows = tok * n_head
    key_dim = queries.shape[1] // n_head
    value_dim = values.shape[1] // n_head
    width = value_dim // CHUNKS
    part = key_dim // MEMBERS
    n_group = n_seq // MEMBERS
    bf16, f32 = jnp.bfloat16, jnp.float32
    n_sem = 5 + 4 * CHUNKS + (n_group - 1) * (1 + CHUNKS)
    scratch = [
        pltpu.VMEM((2, 1, rows), f32),
        pltpu.VMEM((rows, key_dim), bf16),
        pltpu.VMEM((rows, key_dim), bf16),
        pltpu.VMEM((CHUNKS, rows, width), bf16),
        pltpu.VMEM((key_dim, rows), bf16),
        pltpu.VMEM((rows, 1), f32),
        pltpu.VMEM((rows, 1), f32),
        pltpu.VMEM((rows, 1), f32),
        pltpu.VMEM((rows, rows), f32),
        pltpu.VMEM((rows, rows), bf16),
        pltpu.VMEM((rows, 2), f32),
        pltpu.VMEM((CHUNKS, rows, width), f32),
        pltpu.VMEM((8, 128), f32),
        pltpu.VMEM((MEMBERS, 8, 128), f32),
        pltpu.VMEM((8, 128), f32),
        pltpu.VMEM((MEMBERS, 8, 128), f32),
        pltpu.VMEM((8, 128), f32),
        pltpu.VMEM((n_group, 8, 128), f32),
        pltpu.VMEM((MEMBERS, 8, 128), f32),
        pltpu.VMEM((MEMBERS, 8, 128), f32),
        pltpu.VMEM((MEMBERS, 8, 128), f32),
        pltpu.VMEM((n_group, 8, 128), f32),
        pltpu.VMEM((CHUNKS, MEMBERS, part, width), bf16),
        pltpu.VMEM((CHUNKS, MEMBERS, part, width), bf16),
        pltpu.VMEM((CHUNKS, part, width), bf16),
        pltpu.VMEM((CHUNKS, part, width), bf16),
        pltpu.VMEM((CHUNKS, n_group, part, width), bf16),
        pltpu.VMEM((CHUNKS, MEMBERS, part, width), bf16),
        pltpu.VMEM((CHUNKS, key_dim, width), bf16),
        pltpu.VMEM((CHUNKS, rows, width), bf16),
        pltpu.SemaphoreType.DMA((n_sem,)),
        pltpu.SemaphoreType.DMA((n_sem,)),
        pltpu.SemaphoreType.REGULAR,
    ]
    anywhere = pl.BlockSpec(memory_space=pl.ANY)
    hbm = pl.BlockSpec(memory_space=pltpu.HBM)
    returned = pl.pallas_call(
        functools.partial(kernel, (n_seq, n_head)),
        out_shape=pltpu.VMEM((tok, n_head * value_dim), bf16),
        in_specs=[hbm] * 5,
        out_specs=pl.BlockSpec(memory_space=pltpu.VMEM),
        scratch_shapes=scratch,
        compiler_params=pltpu.CompilerParams(
            collective_id=0, has_side_effects=True, vmem_limit_bytes=60 * 2**20
        ),
    )(queries, keys, values, in_gate, forget_gate)
    gated = jax.nn.sigmoid(out_gate.astype(f32)) * returned.astype(f32)
    return gated.astype(bf16)


def solution(mesh):
    return jax.shard_map(
        functools.partial(per_device, mesh.shape["seq"], mesh.shape["head"]),
        mesh=mesh,
        in_specs=(
            P(("seq", "head"), None),
            P(("seq", "head"), None),
            P(("seq", "head"), None),
            P("head", "seq"),
            P("head", "seq"),
            P(("seq", "head"), None),
        ),
        out_specs=P(("seq", "head"), None),
        check_vma=False,
    )
```

```python
import functools

import jax
import jax.numpy as jnp
from jax import lax
from jax.experimental import pallas as pl
from jax.experimental.pallas import tpu as pltpu
from jax.sharding import PartitionSpec as P

MESH = pl.DeviceIdType.MESH
NEG_FILL = -1e30
MEMBERS = 16
CHUNKS = 4
ROW = 4
TILE = 128
LAG = 2
PEERS = ((2, 0), (1, 0), (3, 0), (2, 1), (1, 1), (3, 1), (0, 1))


def kernel(
    sizes,
    q_ref,
    k_ref,
    v_ref,
    ig_ref,
    fg_ref,
    ret_ref,
    gates,
    qbuf,
    kbuf,
    vbuf,
    wkt,
    within_col,
    weight_col,
    local_max,
    scores,
    mixing,
    entry_rate,
    local_out,
    hdr,
    hdr_all,
    nrm,
    nrm_all,
    hdr_total,
    hdr_total_all,
    coef_local,
    coef_full,
    entry,
    coef_total,
    mown,
    mrecv,
    usend,
    umerged,
    urecv,
    isend,
    irecv,
    hid,
    send_sem,
    recv_sem,
    relay_sem,
    row_sem,
):
    n_seq, n_head = sizes
    n_group = n_seq // MEMBERS
    tok = q_ref.shape[0]
    rows, key_dim = kbuf.shape
    width = vbuf.shape[2]
    value_dim = width * CHUNKS
    part = key_dim // MEMBERS
    seq = lax.axis_index("seq")
    head = lax.axis_index("head")
    me = lax.rem(seq, MEMBERS)
    group = seq // MEMBERS
    base = group * MEMBERS
    head_row = pl.multiple_of(head * tok, tok)

    later = n_group - 1
    K, Q, HDR, NRM, GATE = range(5)
    V, A, C, R = (5 + CHUNKS * i for i in range(4))
    HDRT = 5 + 4 * CHUNKS
    B = HDRT + later

    turned = jnp.where(group == later, MEMBERS // 2, 0)
    mine = lax.rem(me + turned, MEMBERS)

    def member(j):
        return base + lax.rem(me + j, MEMBERS)

    def owner_later(j):
        turn = jnp.where(group + j == later, MEMBERS // 2, 0)
        return (group + j) * MEMBERS + lax.rem(me + turn, MEMBERS)

    def each_later(act):
        for j in (2, 3, 1):
            pl.when(group + j < n_group)(functools.partial(act, j, owner_later(j)))

    def each_earlier(act):
        for j in range(later):
            pl.when(j < group)(functools.partial(act, j, j * MEMBERS + mine))

    def takes(j):
        return ((group == 1) | (group == 3), group >= 2, group == 3)[j]

    def total_arrived(c, j):
        arrived(urecv.at[c, j], B + later * c + j)

    def peer(j):
        chip, flip = PEERS[j - 1]
        core = lax.rem(head, 2)
        there = lax.rem(head // 2 + chip, n_head // 2)
        return 2 * there + (1 - core if flip else core)

    def put(src, dst, which, device, lands=None):
        pltpu.make_async_remote_copy(
            src_ref=src,
            dst_ref=dst,
            send_sem=send_sem.at[which],
            recv_sem=recv_sem.at[which if lands is None else lands],
            device_id=device,
            device_id_type=MESH,
        ).start()

    def arrived(ref, which):
        pltpu.make_async_copy(ref, ref, recv_sem.at[which]).wait()

    def sent(ref, which):
        pltpu.make_async_copy(ref, ref, send_sem.at[which]).wait()

    def local(src, dst, which):
        pltpu.make_async_copy(src, dst, recv_sem.at[which]).start()

    local(ig_ref, gates.at[0], GATE)
    local(fg_ref, gates.at[1], GATE)

    barrier = pltpu.get_barrier_semaphore()

    def greet(j, there):
        pl.semaphore_signal(barrier, inc=1, device_id=(there, head), device_id_type=MESH)

    each_later(greet)
    for j in range(ROW, MEMBERS, ROW):
        pl.semaphore_signal(barrier, inc=1, device_id=(member(j), head), device_id_type=MESH)
    for j in range(1, ROW):
        beside = base + me - lax.rem(me, ROW) + lax.rem(me + j, ROW)
        pl.semaphore_signal(barrier, inc=1, device_id=(beside, head), device_id_type=MESH)
    for j in range(1, n_head):
        pl.semaphore_signal(barrier, inc=1, device_id=(seq, peer(j)), device_id_type=MESH)

    def key_cols(h):
        return pl.ds(pl.multiple_of(h * key_dim, key_dim), key_dim)

    def value_cols(h, c):
        return pl.ds(pl.multiple_of(h * value_dim + c * width, width), width)

    my_rows = pl.ds(head_row, tok)
    local(k_ref.at[:, key_cols(head)], kbuf.at[my_rows], K)
    for c in range(CHUNKS):
        local(v_ref.at[:, value_cols(head, c)], vbuf.at[c, my_rows], V + c)
    local(q_ref.at[:, key_cols(head)], qbuf.at[my_rows], Q)

    for j in range(later):

        @pl.when(j >= group)
        def _():
            hdr_total_all[j] = jnp.zeros(hdr_total.shape, jnp.float32)

        @pl.when(jnp.logical_not(takes(j)))
        def _():
            for c in range(CHUNKS):
                urecv[c, j] = jnp.zeros(urecv.shape[2:], urecv.dtype)

    rows_apart = MEMBERS // ROW - 1
    pl.semaphore_wait(barrier, n_head - 1 + rows_apart + ROW - 1 + group)

    for j in range(ROW, MEMBERS, ROW):
        pl.semaphore_signal(row_sem, inc=1, device_id=(member(j), head), device_id_type=MESH)

    def answer(j, there):
        pl.semaphore_signal(relay_sem, inc=1, device_id=(there, head), device_id_type=MESH)

    each_earlier(answer)

    for j in range(1, n_head):
        h = peer(j)
        put(k_ref.at[:, key_cols(h)], kbuf.at[my_rows], K, (seq, h))
    for c in range(CHUNKS):
        for j in range(1, n_head):
            h = peer(j)
            put(v_ref.at[:, value_cols(h, c)], vbuf.at[c, my_rows], V + c, (seq, h))
    arrived(gates, GATE)
    gate = gates[0]
    forget = gates[1]
    log_keep = jnp.minimum(forget, 0.0) - jnp.log1p(jnp.exp(-jnp.abs(forget)))
    lane = lax.broadcasted_iota(jnp.int32, (8, rows), 1)
    within_row = jnp.broadcast_to(log_keep, (8, rows))
    step = 1
    while step < rows:
        within_row = within_row + jnp.where(lane >= step, pltpu.roll(within_row, step, 1), 0.0)
        step *= 2
    within_row = within_row[0:1, :]
    decay = within_row[:, rows - 1 : rows]
    gate_less = gate - within_row

    def gate_tile(i, peak):
        at = pl.ds(pl.multiple_of(i * TILE, TILE), TILE)
        t = lax.broadcasted_iota(jnp.int32, (TILE, rows), 0) + i * TILE
        s = lax.broadcasted_iota(jnp.int32, (TILE, rows), 1)
        col = jnp.sum(jnp.where(s <= t, log_keep, 0.0), axis=1, keepdims=True)
        own_gate = jnp.sum(jnp.where(s == t, gate, 0.0), axis=1, keepdims=True)
        since = decay - col + own_gate
        within_col[at, :] = col
        weight_col[at, :] = since
        local_max[at, :] = col + jnp.max(
            jnp.where(s <= t, gate_less, NEG_FILL), axis=1, keepdims=True
        )
        return jnp.maximum(peak, jnp.max(since, axis=0, keepdims=True))

    peak_own = lax.fori_loop(
        0, rows // TILE, gate_tile, jnp.full((1, 1), -jnp.inf, jnp.float32)
    )
    hdr[...] = jnp.zeros_like(hdr)
    hdr[0:1, :] = jnp.broadcast_to(decay, (1, 128))
    hdr[1:2, :] = jnp.broadcast_to(peak_own, (1, 128))
    hdr_total[...] = jnp.zeros_like(hdr_total)
    nrm[...] = jnp.zeros_like(nrm)
    hdr_all[me] = hdr[...]
    pl.semaphore_wait(row_sem, rows_apart)
    for j in range(1, MEMBERS):
        put(hdr, hdr_all.at[me], HDR, (member(j), head))

    arrived(kbuf, K)

    def key_tile(i, normal):
        at = pl.ds(pl.multiple_of(i * TILE, TILE), TILE)
        weight = jnp.exp(weight_col[at, :] - peak_own)
        weighted = weight * kbuf[at, :].astype(jnp.float32)
        wkt[:, at] = weighted.T.astype(jnp.bfloat16)
        return normal + jnp.sum(weighted, axis=0, keepdims=True)

    normal_own = lax.fori_loop(
        0, rows // TILE, key_tile, jnp.zeros((1, key_dim), jnp.float32)
    )
    for i in range(key_dim // 128):
        nrm[2 + i : 3 + i, :] = normal_own[:, i * 128 : (i + 1) * 128]
    nrm_all[me] = nrm[...]
    for j in range(1, MEMBERS):
        put(nrm, nrm_all.at[me], NRM, (member(j), head))

    norm_rows = slice(2, 2 + key_dim // 128)
    no_peak = jnp.full((1, 128), NEG_FILL, jnp.float32)
    no_norm = jnp.zeros((key_dim // 128, 128), jnp.float32)

    arrived(hdr_all.at[pl.ds(0, MEMBERS - 1)], HDR)
    peak, total = no_peak, jnp.zeros((1, 128), jnp.float32)
    for g in range(MEMBERS):
        d, p = hdr_all[g, 0:1, :], hdr_all[g, 1:2, :]
        new = jnp.maximum(d + peak, p)
        coef_local[g, 0:1, :] = jnp.exp(d + peak - new)
        coef_local[g, 1:2, :] = jnp.exp(p - new)
        peak, total = new, total + d
    hdr_total[0:1, :] = total
    hdr_total[1:2, :] = peak

    for c in range(CHUNKS):
        arrived(vbuf.at[c], V + c)
        own = jnp.dot(wkt[...], vbuf[c], preferred_element_type=jnp.float32)
        mown[c] = own.astype(jnp.bfloat16).reshape(MEMBERS, part, width)
        for j in range(1, MEMBERS):
            g = lax.rem(me + j, MEMBERS)
            owned = lax.rem(g + turned, MEMBERS)
            put(mown.at[c, owned], mrecv.at[c, me], A + c, (base + g, head))
        mrecv[c, me] = mown[c, mine]
        if c == CHUNKS - 2:
            for j in range(1, n_head):
                h = peer(j)
                put(q_ref.at[:, key_cols(h)], qbuf.at[my_rows], Q, (seq, h))

    arrived(nrm_all.at[pl.ds(0, MEMBERS - 1)], NRM)
    norm = no_norm
    for g in range(MEMBERS):
        norm = coef_local[g, 0:1, :] * norm + coef_local[g, 1:2, :] * nrm_all[g, norm_rows, :]
    hdr_total[norm_rows, :] = norm
    hdr_total_all[group] = hdr_total[...]

    @pl.when(group < later)
    def _():
        pl.semaphore_wait(relay_sem, later - group)

    def send_header(j, there):
        put(hdr_total, hdr_total_all.at[group], HDRT + j - 1, (there, head), HDRT + group)

    each_later(send_header)

    scale = key_dim ** (-0.5)

    def score_tile(i, carry):
        at = pl.ds(pl.multiple_of(i * TILE, TILE), TILE)
        scores[at, :] = lax.dot_general(
            qbuf[at, :], kbuf[...], (((1,), (1,)), ((), ())), preferred_element_type=jnp.float32
        )
        return carry

    def wide(row):
        return jnp.concatenate([row] * (width // 128), axis=1)

    def full_headers():
        each_earlier(lambda j, there: arrived(hdr_total_all.at[j], HDRT + j))
        peak, norm = no_peak, no_norm
        for j in range(n_group - 1):
            d, p = hdr_total_all[j, 0:1, :], hdr_total_all[j, 1:2, :]
            new = jnp.maximum(d + peak, p)
            used = j < group
            older, newer = jnp.exp(d + peak - new), jnp.exp(p - new)
            coef_total[j, 0:1, :] = older
            coef_total[j, 1:2, :] = newer
            norm = jnp.where(used, older * norm + newer * hdr_total_all[j, norm_rows, :], norm)
            peak = jnp.where(used, new, peak)
        for g in range(MEMBERS):
            entry[g, 1:2, :] = peak
            entry[g, norm_rows, :] = norm
            d, p = hdr_all[g, 0:1, :], hdr_all[g, 1:2, :]
            new = jnp.maximum(d + peak, p)
            older, newer = jnp.exp(d + peak - new), jnp.exp(p - new)
            coef_full[g, 0:1, :] = older
            coef_full[g, 1:2, :] = newer
            norm = older * norm + newer * nrm_all[g, norm_rows, :]
            peak = new

    def send_totals(c):
        arrived(mrecv.at[c, pl.ds(0, MEMBERS - 1)], A + c)

        @pl.when(group < later)
        def _():
            state = jnp.zeros((part, width), jnp.float32)
            for g in range(MEMBERS):
                state = (
                    wide(coef_local[g, 0:1, :]) * state
                    + wide(coef_local[g, 1:2, :]) * mrecv[c, g].astype(jnp.float32)
                )
            usend[c] = state.astype(jnp.bfloat16)

            def send_total(src, j):
                at = B + later * c
                put(src, urecv.at[c, group], at + j - 1, (owner_later(j), head), at + group)

            pl.when(group == 0)(functools.partial(send_total, usend.at[c], 3))
            pl.when(group == 1)(functools.partial(send_total, usend.at[c], 2))
            pl.when(group != 1)(functools.partial(send_total, usend.at[c], 1))

            @pl.when(group == 1)
            def _():
                total_arrived(c, 0)
                umerged[c] = (
                    wide(coef_total[1, 0:1, :]) * urecv[c, 0].astype(jnp.float32)
                    + wide(coef_total[1, 1:2, :]) * state
                ).astype(jnp.bfloat16)
                send_total(umerged.at[c], 1)

    def send_entering(c):
        pl.when(group == 3)(functools.partial(total_arrived, c, 0))
        for j in range(1, later):
            pl.when(takes(j))(functools.partial(total_arrived, c, j))
        came = [urecv[c, j].astype(jnp.float32) for j in range(later)]
        every = came[0]
        for j in range(1, later):
            every = wide(coef_total[j, 0:1, :]) * every + wide(coef_total[j, 1:2, :]) * came[j]
        state = jnp.where(group == 3, every, jnp.where(group == 2, came[1], came[0]))
        for g in range(MEMBERS):
            isend[c, g] = state.astype(jnp.bfloat16)
            state = (
                wide(coef_full[g, 0:1, :]) * state
                + wide(coef_full[g, 1:2, :]) * mrecv[c, g].astype(jnp.float32)
            )
        my_part = pl.ds(pl.multiple_of(mine * part, part), part)
        for j in range(1, MEMBERS):
            g = lax.rem(me + j, MEMBERS)
            put(isend.at[c, g], irecv.at[c, my_part], C + c, (base + g, head))
        irecv[c, my_part] = isend[c, me]

    pl.when(group < 2)(full_headers)
    for c in range(CHUNKS):
        send_totals(c)
        if c >= LAG:
            pl.when(group < 2)(functools.partial(send_entering, c - LAG))
    pl.when(group >= 2)(full_headers)
    arrived(qbuf, Q)
    pl.when(group == 3)(lambda: lax.fori_loop(0, rows // TILE, score_tile, None))
    for c in range(CHUNKS):
        if c >= CHUNKS - LAG:
            send_entering(c)
        else:
            pl.when(group >= 2)(functools.partial(send_entering, c))
    pl.when(group < 3)(lambda: lax.fori_loop(0, rows // TILE, score_tile, None))

    my_entry = entry[me]
    peak_in = my_entry[1:2, 0:1]
    normal_in = jnp.concatenate(
        [my_entry[2 + i : 3 + i, :] for i in range(key_dim // 128)], axis=1
    )

    def mixing_tile(i, carry):
        at = pl.ds(pl.multiple_of(i * TILE, TILE), TILE)
        t = lax.broadcasted_iota(jnp.int32, (TILE, rows), 0) + i * TILE
        s = lax.broadcasted_iota(jnp.int32, (TILE, rows), 1)
        col = within_col[at, :]
        entry_log = col + peak_in
        peak_row = jnp.maximum(entry_log, local_max[at, :])
        logs = jnp.where(s <= t, (col - peak_row) + gate_less, NEG_FILL)
        mix = jnp.exp(logs) * (scores[at, :] * scale)
        mixing[at, :] = mix.astype(jnp.bfloat16)
        rate = jnp.exp(entry_log - peak_row)
        from_normal = jnp.sum(
            qbuf[at, :].astype(jnp.float32) * normal_in, axis=1, keepdims=True
        )
        below = jnp.sum(mix, axis=1, keepdims=True) + rate * (from_normal * scale)
        inverse = 1.0 / jnp.maximum(jnp.abs(below), 1.0)
        entry_rate[at, 0:1] = rate * inverse * scale
        entry_rate[at, 1:2] = inverse
        return carry

    lax.fori_loop(0, rows // TILE, mixing_tile, 0)

    def local_tile(i, carry):
        at = pl.ds(pl.multiple_of(i * TILE, TILE), TILE)
        for c in range(CHUNKS):
            local_out[c, at, :] = entry_rate[at, 1:2] * jnp.dot(
                mixing[at, :], vbuf[c], preferred_element_type=jnp.float32
            )
        return carry

    lax.fori_loop(0, rows // TILE, local_tile, 0)

    def send_hidden(c, h):
        put(
            hid.at[c, pl.ds(pl.multiple_of(h * tok, tok), tok)],
            ret_ref.at[:, value_cols(head, c)],
            R + c,
            (seq, h),
        )

    for c in range(CHUNKS):
        arrived(irecv.at[c, pl.ds(0, key_dim - part)], C + c)

        for i in range(n_head // 2 - 1, -1, -1):
            chip = lax.rem(head // 2 + (i + 1) % (n_head // 2), n_head // 2)
            at = pl.ds(pl.multiple_of(chip * 2 * tok, 2 * tok), 2 * tok)
            from_memory = jnp.dot(
                qbuf[at, :], irecv[c], preferred_element_type=jnp.float32
            )
            hid[c, at, :] = (
                local_out[c, at, :] + entry_rate[at, 0:1] * from_memory
            ).astype(jnp.bfloat16)
            for core in range(2):
                h = 2 * chip + core
                pl.when(h != head)(functools.partial(send_hidden, c, h))
        local(hid.at[c, my_rows], ret_ref.at[:, value_cols(head, c)], R + c)

    for c in range(CHUNKS):
        arrived(hid.at[c], R + c)

    peers_rows = pl.ds(0, rows - tok)
    sent(kbuf.at[peers_rows], K)
    sent(qbuf.at[peers_rows], Q)
    sent(hdr_all.at[pl.ds(0, MEMBERS - 1)], HDR)
    sent(nrm_all.at[pl.ds(0, MEMBERS - 1)], NRM)
    each_later(lambda j, there: sent(hdr_total, HDRT + j - 1))
    for c in range(CHUNKS):
        sent(vbuf.at[c, peers_rows], V + c)
        sent(mrecv.at[c, pl.ds(0, MEMBERS - 1)], A + c)
        pl.when(group < later)(lambda: sent(usend.at[c], B + later * c))
        pl.when(group == 1)(lambda: sent(usend.at[c], B + later * c + 1))
        pl.when(group == 0)(lambda: sent(usend.at[c], B + later * c + 2))
        sent(irecv.at[c, pl.ds(0, key_dim - part)], C + c)
        sent(hid.at[c, peers_rows], R + c)


def per_device(n_seq, n_head, queries, keys, values, in_gate, forget_gate, out_gate):
    tok = queries.shape[0]
    rows = tok * n_head
    key_dim = queries.shape[1] // n_head
    value_dim = values.shape[1] // n_head
    width = value_dim // CHUNKS
    part = key_dim // MEMBERS
    n_group = n_seq // MEMBERS
    bf16, f32 = jnp.bfloat16, jnp.float32
    n_sem = 5 + 4 * CHUNKS + (n_group - 1) * (1 + CHUNKS)
    scratch = [
        pltpu.VMEM((2, 1, rows), f32),
        pltpu.VMEM((rows, key_dim), bf16),
        pltpu.VMEM((rows, key_dim), bf16),
        pltpu.VMEM((CHUNKS, rows, width), bf16),
        pltpu.VMEM((key_dim, rows), bf16),
        pltpu.VMEM((rows, 1), f32),
        pltpu.VMEM((rows, 1), f32),
        pltpu.VMEM((rows, 1), f32),
        pltpu.VMEM((rows, rows), f32),
        pltpu.VMEM((rows, rows), bf16),
        pltpu.VMEM((rows, 2), f32),
        pltpu.VMEM((CHUNKS, rows, width), f32),
        pltpu.VMEM((8, 128), f32),
        pltpu.VMEM((MEMBERS, 8, 128), f32),
        pltpu.VMEM((8, 128), f32),
        pltpu.VMEM((MEMBERS, 8, 128), f32),
        pltpu.VMEM((8, 128), f32),
        pltpu.VMEM((n_group, 8, 128), f32),
        pltpu.VMEM((MEMBERS, 8, 128), f32),
        pltpu.VMEM((MEMBERS, 8, 128), f32),
        pltpu.VMEM((MEMBERS, 8, 128), f32),
        pltpu.VMEM((n_group, 8, 128), f32),
        pltpu.VMEM((CHUNKS, MEMBERS, part, width), bf16),
        pltpu.VMEM((CHUNKS, MEMBERS, part, width), bf16),
        pltpu.VMEM((CHUNKS, part, width), bf16),
        pltpu.VMEM((CHUNKS, part, width), bf16),
        pltpu.VMEM((CHUNKS, n_group, part, width), bf16),
        pltpu.VMEM((CHUNKS, MEMBERS, part, width), bf16),
        pltpu.VMEM((CHUNKS, key_dim, width), bf16),
        pltpu.VMEM((CHUNKS, rows, width), bf16),
        pltpu.SemaphoreType.DMA((n_sem,)),
        pltpu.SemaphoreType.DMA((n_sem,)),
        pltpu.SemaphoreType.REGULAR,
        pltpu.SemaphoreType.REGULAR,
    ]
    anywhere = pl.BlockSpec(memory_space=pl.ANY)
    hbm = pl.BlockSpec(memory_space=pltpu.HBM)
    returned = pl.pallas_call(
        functools.partial(kernel, (n_seq, n_head)),
        out_shape=pltpu.VMEM((tok, n_head * value_dim), bf16),
        in_specs=[hbm] * 5,
        out_specs=pl.BlockSpec(memory_space=pltpu.VMEM),
        scratch_shapes=scratch,
        compiler_params=pltpu.CompilerParams(
            collective_id=0, has_side_effects=True, vmem_limit_bytes=60 * 2**20
        ),
    )(queries, keys, values, in_gate, forget_gate)
    gated = jax.nn.sigmoid(out_gate.astype(f32)) * returned.astype(f32)
    return gated.astype(bf16)


def solution(mesh):
    return jax.shard_map(
        functools.partial(per_device, mesh.shape["seq"], mesh.shape["head"]),
        mesh=mesh,
        in_specs=(
            P(("seq", "head"), None),
            P(("seq", "head"), None),
            P(("seq", "head"), None),
            P("head", "seq"),
            P("head", "seq"),
            P(("seq", "head"), None),
        ),
        out_specs=P(("seq", "head"), None),
        check_vma=False,
    )
```
